256 devices in a mesh: dp: 16 (over z, y_hi), seq: 16 (over x, y_lo, core).
Axes of the slice: x: 4, y: 4 (y_hi: 2, y_lo: 2; y = y_hi * 2 + y_lo), z: 8, core: 2. Of those that a mesh axis runs over, the one named last changes fastest.
Arguments:
- tokens: bfloat16 [16, 4096, 768], P('dp', 'seq'), may hold values from -6 to 6
- cotangent: bfloat16 [16, 4096, 768], P('dp', 'seq'), may hold values from -6 to 6
- w_conv: bfloat16 [3, 768, 512], P(None, ('dp', 'seq')), may hold values from -0.125 to 0.125
- w_point: bfloat16 [512, 768], P(('dp', 'seq')), may hold values from -0.25 to 0.25
Outputs:
- output: bfloat16 [16, 4096, 768], P('dp', 'seq')
- grad_tokens: bfloat16 [16, 4096, 768], P('dp', 'seq')
- grad_conv: float32 [768, 3, 512], P(('dp', 'seq'))
- grad_point: float32 [512, 768], P(('dp', 'seq'))
The draws below stay inside these ranges and needn't reach their ends.
All inputs are finite; a program needn't handle non-finite values.
Results may differ from the reference program's by a relative error of at most 0.0052.
Values may be sent and summed in bfloat16 or wider, within the bound.
No kernel may reach another device: no remote copies, remote signals or barrier semaphores. Data moves between devices by JAX's collectives and lax.ppermute only.
A program may use at most 64 MiB of HBM per device.

```python
import jax
import jax.numpy as jnp

D = 768
INNER = 512
BATCH = 16
BINS = 4096
DILATION = 1024


def raised(result, key, source, target, parts, factor):
    def block_of(dim):
        return (jnp.arange(result.shape[dim]) // (result.shape[dim] // parts)).reshape((-1,) + (1,) * (result.ndim - 1 - dim))

    one_side = jax.random.permutation(key, parts)[block_of(target)]
    other_side = (block_of(target) + parts // 2) % parts
    return jnp.where((block_of(source) == one_side) | (block_of(source) == other_side), factor * result, result)


def steps_of(key, shape, cuts, smallest, top_value):
    gain, own = 1.0, jax.random.fold_in(key, 6)
    for dim, blocks in cuts:
        heights = jnp.exp(jax.random.uniform(jax.random.fold_in(own, dim), (blocks,), jnp.float32, smallest / len(cuts), top_value / len(cuts)))
        gain = gain * jnp.repeat(heights, shape[dim] // blocks).reshape([-1 if axis == dim else 1 for axis in range(len(shape))])
    return gain


def bell_draw(own_key, dims, width, most, shards=(), kind=jnp.bfloat16):
    factor_of = steps_of(own_key, dims, shards, -0.22, 0.18) if shards else 1.0
    drawn = jax.random.normal(own_key, dims, jnp.float32) * width * factor_of
    return jnp.minimum(jnp.maximum(drawn, -most), most).astype(kind)


def bell_draw_with(own_key, shape, scale, bound, shards, heavy, held_as=jnp.bfloat16):
    values = scale * jax.random.normal(own_key, shape, jnp.float32)
    if shards:
        values = values * steps_of(own_key, shape, shards, -0.22, 0.18)
    return jnp.clip(raised(values, jax.random.fold_in(own_key, 3), *heavy), -bound, bound).astype(held_as)


def setup_inputs(seed: int = 0) -> dict:
    key_list = jax.random.split(jax.random.key(seed), 5)
    return {
        "tokens": bell_draw_with(key_list[0], (BATCH, BINS, D), 1.0, 6.0, ((0, 16), (1, 16)), (1, 2, 16, 2.0)),
        "cotangent": bell_draw(key_list[1], (BATCH, BINS, D), 1.0, 6.0, ((0, 16), (1, 16))),
        "w_conv": bell_draw(key_list[2], (3, D, INNER), (3 * D) ** -0.5, 0.125, ((1, 256),)),
        "w_point": bell_draw(key_list[3], (INNER, D), INNER ** -0.5, 0.25, ((0, 256),)),
    }


def gelu_tanh(values):
    return jax.nn.gelu(values, approximate=True)

def reference(tokens, cotangent, w_conv, w_point):
    tokens_wide = tokens.astype(jnp.float32)
    activated = gelu_tanh(tokens_wide).astype(jnp.bfloat16)
    padded = jnp.pad(activated, ((0, 0), (DILATION, DILATION), (0, 0)))
    before = padded[:, :BINS]
    after = padded[:, 2 * DILATION:]
    taps = [before, activated, after]
    conv_wide = w_conv.astype(jnp.float32)
    conv_out = jnp.zeros((BATCH, BINS, INNER), jnp.float32)
    for index in range(3):
        conv_out = conv_out + jnp.einsum('bsd,dh->bsh', taps[index].astype(jnp.float32), conv_wide[index])
    inner_act = gelu_tanh(conv_out).astype(jnp.bfloat16)
    point_wide = w_point.astype(jnp.float32)
    inner_wide = inner_act.astype(jnp.float32)
    output = (tokens_wide + jnp.einsum('bsh,hd->bsd', inner_wide, point_wide)).astype(jnp.bfloat16)
    grad_out = cotangent.astype(jnp.float32)
    grad_point = jnp.einsum('bsh,bsd->hd', inner_wide, grad_out)
    grad_pre = jnp.einsum('bsd,hd->bsh', grad_out, point_wide)
    grad_inner = jax.vjp(gelu_tanh, conv_out)[1](grad_pre)[0].astype(jnp.bfloat16)
    inner_grad_wide = grad_inner.astype(jnp.float32)
    grad_conv = jnp.stack([jnp.einsum('bsd,bsh->dh', taps[index].astype(jnp.float32), inner_grad_wide) for index in range(3)], axis=1)
    grad_padded = jnp.pad(inner_grad_wide, ((0, 0), (DILATION, DILATION), (0, 0)))
    grad_later = grad_padded[:, 2 * DILATION:]
    grad_earlier = grad_padded[:, :BINS]
    grad_act = jnp.einsum('bsh,dh->bsd', grad_later, conv_wide[0])
    grad_act = grad_act + jnp.einsum('bsh,dh->bsd', inner_grad_wide, conv_wide[1])
    grad_act = grad_act + jnp.einsum('bsh,dh->bsd', grad_earlier, conv_wide[2])
    grad_tokens = (grad_out + jax.vjp(gelu_tanh, tokens_wide)[1](grad_act)[0]).astype(jnp.bfloat16)
    return (output, grad_tokens, grad_conv, grad_point)
```

```python
import numpy as np
import jax
import jax.numpy as jnp
from jax import lax
from jax.sharding import Mesh, PartitionSpec as P

NZ, NYH, NX, NYL, NC = 8, 2, 4, 2, 2
AXES = ("z", "yh", "x", "yl", "core")
PLANE = ("yh", "x", "yl")
LINE = ("z", "core")
BF16 = jnp.bfloat16
F32 = jnp.float32


def one_hot_rows(source):
    source = np.asarray(source).reshape(-1)
    matrix = np.zeros((source.size, source.size), np.float32)
    matrix[np.arange(source.size), source] = 1.0
    return matrix


def spread_order():
    rows = np.zeros((NX, 192), np.int64)
    for x in range(NX):
        for t in range(3):
            for zc in range(16):
                for r in range(3):
                    rows[x, t * 48 + zc * 3 + r] = zc * 48 + x * 9 + t * 3 + r
        for j in range(6):
            for z2 in range(2):
                for core in range(2):
                    for r in range(2):
                        zc = (2 * x + z2) * 2 + core
                        rows[x, 144 + j * 8 + z2 * 4 + core * 2 + r] = zc * 48 + 36 + r * 6 + j
    return one_hot_rows(rows)


def channel_order():
    rows = np.zeros((NZ, NYH, NX, NYL, NC, 3), np.int64)
    for z, yh, x, yl, core, r in np.ndindex(*rows.shape):
        rows[z, yh, x, yl, core, r] = ((yh * 4 + x) * 2 + yl) * 48 + (z * 2 + core) * 3 + r
    return one_hot_rows(rows)


def inner_order():
    rows = np.zeros((6, 2, NYH, NX, NYL, NC, 2), np.int64)
    for j, z2, yh, x, yl, core, r in np.ndindex(*rows.shape):
        rows[j, z2, yh, x, yl, core, r] = ((yh * 4 + x) * 2 + yl) * 48 + j * 8 + z2 * 4 + core * 2 + r
    return one_hot_rows(rows)


def step_along_x(value, step):
    return lax.ppermute(value, "x", [(i, (i + step) % NX) for i in range(NX)])


def gelu_tanh(values):
    return jax.nn.gelu(values, approximate=True)


def dot(left, right, left_dim, right_dim):
    return lax.dot_general(
        left, right, (((left_dim,), (right_dim,)), ((), ())), preferred_element_type=F32
    )


def shards(tokens, cotangent, w_conv, w_point):
    me = lax.axis_index("x")
    spread = jnp.asarray(spread_order(), BF16)
    channels = jnp.asarray(channel_order(), BF16)
    inner = jnp.asarray(inner_order(), BF16)

    own = jnp.concatenate(
        [
            w_conv.reshape(3, 3, NX, 128).transpose(2, 0, 1, 3).reshape(36, 128),
            w_point.reshape(12, 128),
        ],
        axis=0,
    )
    line = lax.all_to_all(jnp.broadcast_to(own, (16, 48, 128)), LINE, 0, 0)
    blocks = dot(spread, line.reshape(768, 128), 1, 0).astype(BF16).reshape(NX, 192, 128)

    tokens_wide = tokens[0].astype(F32)
    pair = jnp.stack([gelu_tanh(tokens_wide).astype(BF16), cotangent[0]])
    from_left = step_along_x(pair, 1)
    from_right = step_along_x(pair, -1)
    far_top = step_along_x(from_left[:, :128], 1)
    far_bottom = step_along_x(from_right[:, 128:], -1)
    far = jnp.concatenate([far_top, far_bottom], axis=1)
    both = jnp.concatenate([pair, from_right, far, from_left], axis=1)
    act, grad_out = both[0], both[1]

    plane = lax.all_to_all(
        jnp.broadcast_to(blocks[None, :, None], (NYH, NX, NYL, 192, 128)).reshape(16, 192, 128),
        PLANE, 0, 0,
    )
    conv_rows = jnp.concatenate(
        [plane[:, t * 48:(t + 1) * 48].reshape(768, 128) for t in range(3)], axis=1
    )
    conv_w = dot(channels, conv_rows, 1, 0).astype(BF16)
    point_w = dot(inner, plane[:, 144:].reshape(768, 128), 1, 0).astype(BF16)
    point_w = point_w.reshape(6, 128, 128).transpose(1, 0, 2).reshape(128, 768)

    taps = dot(act, conv_w, 1, 0).reshape(4, 256, 384)
    place = [(me + r) % NX for r in range(NX)]
    has_before = [p != 0 for p in place]
    has_after = [p != NX - 1 for p in place]
    conv_out = jnp.concatenate(
        [
            taps[r, :, 128:256]
            + jnp.where(has_before[r], taps[(r - 1) % NX, :, :128], 0.0)
            + jnp.where(has_after[r], taps[(r + 1) % NX, :, 256:], 0.0)
            for r in range(NX)
        ],
        axis=0,
    )
    grad_pre = dot(grad_out, point_w, 1, 1)
    inner_wide, pull = jax.vjp(gelu_tanh, conv_out)
    inner_act = inner_wide.astype(BF16)
    grad_inner = pull(grad_pre)[0].astype(BF16).reshape(4, 256, 128)
    zero = jnp.zeros((), BF16)
    spread_grad = jnp.concatenate(
        [
            jnp.concatenate(
                [
                    jnp.where(has_after[r], grad_inner[(r + 1) % NX], zero),
                    grad_inner[r],
                    jnp.where(has_before[r], grad_inner[(r - 1) % NX], zero),
                ],
                axis=1,
            )
            for r in range(NX)
        ],
        axis=0,
    )
    conv_g = dot(act, spread_grad, 0, 0).astype(BF16)
    point_g = dot(inner_act, grad_out, 0, 0).astype(BF16)
    conv_g = dot(channels, conv_g, 0, 0).astype(BF16).reshape(16, 48, 384)
    point_g = dot(inner, point_g.reshape(128, 6, 128).transpose(1, 0, 2).reshape(768, 128), 0, 0)
    grads = jnp.concatenate(
        [conv_g[:, :, :128], conv_g[:, :, 128:256], conv_g[:, :, 256:],
         point_g.astype(BF16).reshape(16, 48, 128)],
        axis=1,
    )
    plane_g = lax.all_to_all(grads, PLANE, 0, 0)

    out_part = dot(inner_act, point_w, 1, 0).reshape(4, 256, 768)
    act_part = dot(spread_grad, conv_w, 1, 1).reshape(4, 256, 768)
    parts = jnp.stack([out_part, act_part], axis=1)
    top = step_along_x(parts[2, :, :128].astype(BF16), 1).astype(F32)
    bottom = step_along_x(parts[2, :, 128:].astype(BF16), -1).astype(F32)
    to_right = jnp.concatenate([parts[1, :, :128] + top, parts[1, :, 128:]], axis=1)
    to_left = jnp.concatenate([parts[3, :, :128], parts[3, :, 128:] + bottom], axis=1)
    got_left = step_along_x(to_right.astype(BF16), 1).astype(F32)
    got_right = step_along_x(to_left.astype(BF16), -1).astype(F32)
    total = parts[0] + got_left + got_right
    output = (tokens_wide + total[0]).astype(BF16)
    grad_tokens = (
        cotangent[0].astype(F32) + jax.vjp(gelu_tanh, tokens_wide)[1](total[1])[0]
    ).astype(BF16)

    plane_sum = plane_g.astype(F32).reshape(NYH, NX, NYL, 192, 128).sum(axis=(0, 2))
    line_g = dot(spread, plane_sum.astype(BF16).reshape(768, 128), 0, 0).astype(BF16)
    line_g = lax.all_to_all(line_g.reshape(16, 48, 128), LINE, 0, 0)
    share = line_g.astype(F32).sum(axis=0)
    conv_share = share[:36].reshape(NX, 3, 3, 128).transpose(2, 1, 0, 3).reshape(3, 3, 512)
    point_share = share[36:].reshape(2, 768)
    return (output[None], grad_tokens[None], conv_share, point_share)


def solution(mesh):
    fine = Mesh(mesh.devices.reshape(NZ, NYH, NX, NYL, NC), AXES)
    dp, seq = ("z", "yh"), ("x", "yl", "core")
    rows = P(dp, seq, None)
    return jax.shard_map(
        shards,
        mesh=fine,
        in_specs=(rows, rows, P(None, AXES, None), P(AXES, None)),
        out_specs=(rows, rows, P(AXES, None, None), P(AXES, None)),
        check_vma=False,
    )
```

```python
import numpy as np
import jax
import jax.numpy as jnp
from jax import lax
from jax.experimental import pallas as pl
from jax.experimental.pallas import tpu as pltpu
from jax.sharding import Mesh, PartitionSpec as P

NZ, NYH, NX, NYL, NC = 8, 2, 4, 2, 2
AXES = ("z", "yh", "x", "yl", "core")
PLANE = ("yh", "x", "yl")
LINE = ("z", "core")
ROWS, D, TAKE = 256, 768, 128
BF16 = jnp.bfloat16
F32 = jnp.float32
SCALE = 0.7978845608028654
CUBIC = 0.044715


def one_hot_rows(source):
    source = np.asarray(source).reshape(-1)
    matrix = np.zeros((source.size, source.size), np.float32)
    matrix[np.arange(source.size), source] = 1.0
    return matrix


def spread_order():
    rows = np.zeros((NX, 192), np.int64)
    for x in range(NX):
        for t in range(3):
            for zc in range(16):
                for r in range(3):
                    rows[x, t * 48 + zc * 3 + r] = zc * 48 + x * 9 + t * 3 + r
        for j in range(6):
            for z2 in range(2):
                for core in range(2):
                    for r in range(2):
                        zc = (2 * x + z2) * 2 + core
                        rows[x, 144 + j * 8 + z2 * 4 + core * 2 + r] = zc * 48 + 36 + r * 6 + j
    return one_hot_rows(rows)


def channel_order():
    rows = np.zeros((NZ, NYH, NX, NYL, NC, 3), np.int64)
    for z, yh, x, yl, core, r in np.ndindex(*rows.shape):
        rows[z, yh, x, yl, core, r] = ((yh * 4 + x) * 2 + yl) * 48 + (z * 2 + core) * 3 + r
    return one_hot_rows(rows)


def inner_order():
    rows = np.zeros((6, 2, NYH, NX, NYL, NC, 2), np.int64)
    for j, z2, yh, x, yl, core, r in np.ndindex(*rows.shape):
        rows[j, z2, yh, x, yl, core, r] = ((yh * 4 + x) * 2 + yl) * 48 + j * 8 + z2 * 4 + core * 2 + r
    return one_hot_rows(rows)


def step_along_x(value, step):
    return lax.ppermute(value, "x", [(i, (i + step) % NX) for i in range(NX)])


def tanh_of(values):
    return jnp.tanh(SCALE * (values + CUBIC * (values * values * values)))


def gelu_tanh(values):
    return values * (0.5 * (1.0 + tanh_of(values)))


def gelu_slope(values):
    t = tanh_of(values)
    return 0.5 * (1.0 + t) + (0.5 * values) * ((1.0 - t * t) * (SCALE * (1.0 + 3.0 * CUBIC * (values * values))))


def dot(left, right, left_dim, right_dim):
    return lax.dot_general(
        left, right, (((left_dim,), (right_dim,)), ((), ())), preferred_element_type=F32
    )


def kernel_call(body, out_shapes, scratch=(), flops=0, moved=0, limit=16):
    many = isinstance(out_shapes, (list, tuple))
    vmem = pl.BlockSpec(memory_space=pltpu.VMEM)

    def call(*operands):
        return pl.pallas_call(
            body,
            out_shape=out_shapes,
            in_specs=[vmem] * len(operands),
            out_specs=[vmem] * len(out_shapes) if many else vmem,
            scratch_shapes=list(scratch),
            compiler_params=pltpu.CompilerParams(vmem_limit_bytes=limit * 2**20),
            cost_estimate=pl.CostEstimate(flops=flops, bytes_accessed=moved, transcendentals=0),
        )(*operands)

    return call


def shape(*dims, dtype=BF16):
    return jax.ShapeDtypeStruct(dims, dtype)


def spread_kernel(line, order, out):
    for x in range(NX):
        block = dot(order[x * 192:(x + 1) * 192, :], line[...], 1, 0).astype(BF16)
        for yh in range(NYH):
            for yl in range(NYL):
                out[(yh * NX + x) * NYL + yl] = block


def middle_kernel(
    act0, act1, act2, act3, ct0, ct1, ct2, ct3, plane, to_d, to_h, from_d, from_h,
    grads, inner_act, spread_grad, conv_w, point_w,
    rows_s, point_s, taps_s, grad_s, sum_s,
):
    acts, cts = (act0, act1, act2, act3), (ct0, ct1, ct2, ct3)
    me = lax.axis_index("x")
    place = [lax.rem(me + r, NX) for r in range(NX)]
    keep_before = [(p != 0).astype(F32) for p in place]
    keep_after = [(p != NX - 1).astype(F32) for p in place]

    for p in range(16):
        at = slice(p * 48, (p + 1) * 48)
        for t in range(3):
            rows_s[at, t * TAKE:(t + 1) * TAKE] = plane[p, t * 48:(t + 1) * 48, :]
        point_s[at, :] = plane[p, 144:192, :]
    for k in range(3):
        at = slice(k * 256, (k + 1) * 256)
        conv_w[at, :] = dot(to_d[at, :], rows_s[...], 1, 0).astype(BF16)
    for j in range(6):
        at = slice(j * TAKE, (j + 1) * TAKE)
        point_w[:, at] = dot(to_h[at, :], point_s[...], 1, 0).astype(BF16)

    for r in range(NX):
        taps_s[r] = dot(acts[r][...], conv_w[...], 1, 0)
    for r in range(NX):
        grad_pre = dot(cts[r][...], point_w[...], 1, 1)
        conv_out = (
            taps_s[r, :, TAKE:2 * TAKE]
            + taps_s[(r - 1) % NX, :, :TAKE] * keep_before[r]
            + taps_s[(r + 1) % NX, :, 2 * TAKE:] * keep_after[r]
        )
        t = tanh_of(conv_out)
        cdf = 0.5 * (1.0 + t)
        inner_act[r] = (conv_out * cdf).astype(BF16)
        slope = cdf + (0.5 * conv_out) * (
            (1.0 - t * t) * (SCALE * (1.0 + 3.0 * CUBIC * (conv_out * conv_out)))
        )
        grad_s[r] = (grad_pre * slope).astype(BF16)
    for r in range(NX):
        spread_grad[r, :, :TAKE] = grad_s[(r + 1) % NX] * keep_after[r].astype(BF16)
        spread_grad[r, :, TAKE:2 * TAKE] = grad_s[r]
        spread_grad[r, :, 2 * TAKE:] = grad_s[(r - 1) % NX] * keep_before[r].astype(BF16)

    for t in range(3):
        at = slice(t * TAKE, (t + 1) * TAKE)
        total = dot(spread_grad[0, :, at], acts[0][...], 0, 0)
        for r in range(1, NX):
            total = total + dot(spread_grad[r, :, at], acts[r][...], 0, 0)
        sum_s[at, :] = total.astype(BF16)
    for p in range(4):
        back = dot(from_d[p * 192:(p + 1) * 192, :], sum_s[...], 1, 1).astype(BF16)
        for k in range(4):
            for t in range(3):
                grads[4 * p + k, t * 48:(t + 1) * 48, :] = back[
                    k * 48:(k + 1) * 48, t * TAKE:(t + 1) * TAKE
                ]
    total = dot(inner_act[0], cts[0][...], 0, 0)
    for r in range(1, NX):
        total = total + dot(inner_act[r], cts[r][...], 0, 0)
    for j in range(6):
        at = slice(j * TAKE, (j + 1) * TAKE)
        point_s[at, :] = total[:, at].astype(BF16)
    for p in range(4):
        back = dot(from_h[p * 192:(p + 1) * 192, :], point_s[...], 1, 0).astype(BF16)
        for k in range(4):
            grads[4 * p + k, 144:192, :] = back[k * 48:(k + 1) * 48, :]


def parts_kernel(inner_act, spread_grad, conv_w, point_w, *outs):
    for r in (2, 1, 3, 0):
        outs[r][...] = dot(inner_act[r], point_w[...], 1, 0).astype(BF16)
        outs[NX + r][...] = dot(spread_grad[r], conv_w[...], 1, 1).astype(BF16)


def line_kernel(plane, order, out, sum_s):
    for x in range(NX):
        total = plane[x * NYL].astype(F32)
        for yh in range(NYH):
            for yl in range(NYL):
                if yh or yl:
                    total = total + plane[(yh * NX + x) * NYL + yl].astype(F32)
        sum_s[x * 192:(x + 1) * 192, :] = total.astype(BF16)
    for k in range(4):
        at = slice(k * 192, (k + 1) * 192)
        out[at, :] = dot(order[at, :], sum_s[...], 1, 0).astype(BF16)


def shards(tokens, cotangent, w_conv, w_point):
    spread, channels, inner = spread_order(), channel_order(), inner_order()

    def constant(matrix):
        return jnp.asarray(matrix, BF16)

    own = jnp.concatenate(
        [
            w_conv.reshape(3, 3, NX, TAKE).transpose(2, 0, 1, 3).reshape(36, TAKE),
            w_point.reshape(12, TAKE),
        ],
        axis=0,
    )
    line = lax.all_to_all(jnp.broadcast_to(own, (16, 48, TAKE)), LINE, 0, 0)
    blocks = kernel_call(
        spread_kernel, shape(16, 192, TAKE), flops=2 * D * D * TAKE, moved=3 * 2**20
    )(line.reshape(D, TAKE), constant(spread))
    plane = lax.all_to_all(blocks, PLANE, 0, 0)

    tokens_wide = tokens[0].astype(F32)
    act = [gelu_tanh(tokens_wide).astype(BF16), None, None, None]
    ct = [cotangent[0], None, None, None]
    act[3], act[1] = step_along_x(act[0], 1), step_along_x(act[0], -1)
    ct[3], ct[1] = step_along_x(ct[0], 1), step_along_x(ct[0], -1)
    act[2] = step_along_x(act[3], 1)
    ct[2] = step_along_x(ct[1], -1)

    grads, inner_act, spread_grad, conv_w, point_w = kernel_call(
        middle_kernel,
        [
            shape(16, 192, TAKE),
            shape(NX, ROWS, TAKE),
            shape(NX, ROWS, 3 * TAKE),
            shape(D, 3 * TAKE),
            shape(TAKE, D),
        ],
        scratch=[
            pltpu.VMEM((D, 3 * TAKE), BF16),
            pltpu.VMEM((D, TAKE), BF16),
            pltpu.VMEM((NX, ROWS, 3 * TAKE), F32),
            pltpu.VMEM((NX, ROWS, TAKE), BF16),
            pltpu.VMEM((3 * TAKE, D), BF16),
        ],
        flops=4 * 10**9,
        moved=12 * 2**20,
        limit=32,
    )(
        *act, *ct, plane,
        constant(channels), constant(inner), constant(channels.T), constant(inner.T),
    )
    plane_g = lax.all_to_all(grads, PLANE, 0, 0)

    parts = kernel_call(
        parts_kernel, [shape(ROWS, D)] * 8, flops=10**9, moved=6 * 2**20
    )(inner_act, spread_grad, conv_w, point_w)
    out_part, act_part = parts[:4], parts[4:]
    out_far = step_along_x(out_part[2], 1)
    act_far = step_along_x(act_part[2], -1)
    out_left = step_along_x(out_part[3], -1)
    act_right = step_along_x(act_part[1], 1)
    out_right = step_along_x((out_part[1].astype(F32) + out_far.astype(F32)).astype(BF16), 1)
    act_left = step_along_x((act_part[3].astype(F32) + act_far.astype(F32)).astype(BF16), -1)
    output = (
        tokens_wide + out_part[0].astype(F32) + out_left.astype(F32) + out_right.astype(F32)
    ).astype(BF16)
    grad_act = act_part[0].astype(F32) + act_left.astype(F32) + act_right.astype(F32)
    grad_tokens = (ct[0].astype(F32) + grad_act * gelu_slope(tokens_wide)).astype(BF16)

    line_g = kernel_call(
        line_kernel, shape(D, TAKE), scratch=[pltpu.VMEM((D, TAKE), BF16)],
        flops=2 * D * D * TAKE, moved=3 * 2**20,
    )(plane_g, constant(spread.T))
    line_g = lax.all_to_all(line_g.reshape(16, 48, TAKE), LINE, 0, 0)
    share = line_g.astype(F32).sum(axis=0)
    conv_share = share[:36].reshape(NX, 3, 3, TAKE).transpose(2, 1, 0, 3).reshape(3, 3, 512)
    point_share = share[36:].reshape(2, D)
    return (output[None], grad_tokens[None], conv_share, point_share)


def solution(mesh):
    fine = Mesh(mesh.devices.reshape(NZ, NYH, NX, NYL, NC), AXES)
    dp, seq = ("z", "yh"), ("x", "yl", "core")
    rows = P(dp, seq, None)
    return jax.shard_map(
        shards,
        mesh=fine,
        in_specs=(rows, rows, P(None, AXES, None), P(AXES, None)),
        out_specs=(rows, rows, P(AXES, None, None), P(AXES, None)),
        check_vma=False,
    )
```

```python
import numpy as np
import jax
import jax.numpy as jnp
from jax import lax
from jax.experimental import pallas as pl
from jax.experimental.pallas import tpu as pltpu
from jax.sharding import Mesh, PartitionSpec as P

NZ, NYH, NX, NYL, NC = 8, 2, 4, 2, 2
AXES = ("z", "yh", "x", "yl", "core")
SLAB = ("yh", "yl", "core")
SHEET = ("z", "x")
ROWS, D, INNER, TAKE = 256, 768, 512, 128
BF16 = jnp.bfloat16
F32 = jnp.float32
SCALE = 0.7978845608028654
CUBIC = 0.044715


def one_hot_rows(source):
    source = np.asarray(source).reshape(-1)
    matrix = np.zeros((source.size, source.size), np.float32)
    matrix[np.arange(source.size), source] = 1.0
    return matrix


def column_order():
    return one_hot_rows([
        64 * z + 32 * yh + 8 * x + low
        for x in range(NX) for z in range(NZ) for yh in range(NYH) for low in range(8)
    ])


def conv_rows_order():
    matrix = np.zeros((144, 384), np.float32)
    for t, q, r in np.ndindex(3, 16, 3):
        matrix[t * 48 + q * 3 + r, q * 24 + t * 3 + r] = 1.0
    return matrix


def point_rows_order():
    matrix = np.zeros((96, 192), np.float32)
    for j, z, r in np.ndindex(6, NZ, 2):
        matrix[j * 16 + z * 2 + r, z * 24 + 12 + r * 6 + j] = 1.0
    return matrix


def channel_order():
    return one_hot_rows([
        ((yh * 2 + yl) * 2 + core) * 48 + z * 12 + x * 3 + r
        for z in range(4) for yh in range(NYH) for x in range(NX)
        for yl in range(NYL) for core in range(NC) for r in range(3)
    ])


def inner_order():
    return one_hot_rows([p * 16 + z * 2 + r for z in range(NZ) for p in range(8) for r in range(2)])


def step_along_x(value, step):
    return lax.ppermute(value, "x", [(i, (i + step) % NX) for i in range(NX)])


def tanh_of(values):
    return jnp.tanh(SCALE * (values + CUBIC * (values * values * values)))


def gelu_tanh(values):
    return values * (0.5 * (1.0 + tanh_of(values)))


def gelu_slope(values):
    t = tanh_of(values)
    return 0.5 * (1.0 + t) + (0.5 * values) * ((1.0 - t * t) * (SCALE * (1.0 + 3.0 * CUBIC * (values * values))))


def dot(left, right, left_dim, right_dim):
    return lax.dot_general(
        left, right, (((left_dim,), (right_dim,)), ((), ())), preferred_element_type=F32
    )


def kernel_call(body, out_shapes, scratch=(), flops=0, moved=0, limit=8, far=0, far_out=False):
    many = isinstance(out_shapes, (list, tuple))
    vmem, hbm = pl.BlockSpec(memory_space=pltpu.VMEM), pl.BlockSpec(memory_space=pltpu.HBM)
    out_spec = hbm if far_out else vmem

    def call(*operands):
        return pl.pallas_call(
            body,
            out_shape=out_shapes,
            in_specs=[vmem] * (len(operands) - far) + [hbm] * far,
            out_specs=[out_spec] * len(out_shapes) if many else out_spec,
            scratch_shapes=list(scratch),
            compiler_params=pltpu.CompilerParams(vmem_limit_bytes=limit * 2**20),
            cost_estimate=pl.CostEstimate(flops=flops, bytes_accessed=moved, transcendentals=0),
        )(*operands)

    return call


def shape(*dims, dtype=BF16):
    return jax.ShapeDtypeStruct(dims, dtype)


def fetch(sources, targets, sems, first=0):
    copies = [
        pltpu.make_async_copy(source, target, sems.at[first + k])
        for k, (source, target) in enumerate(zip(sources, targets))
    ]
    for copy in copies:
        copy.start()
    return copies


def own_kernel(w_conv_far, w_point_far, order_far, out, rows_s, block_s, w_conv, w_point, order, sems):
    for copy in fetch((w_conv_far, w_point_far, order_far), (w_conv, w_point, order), sems):
        copy.wait()
    rows_s[...] = jnp.zeros_like(rows_s)
    for t in range(3):
        rows_s[t * 3:(t + 1) * 3, :] = w_conv[t].astype(F32)
    parted = dot(rows_s[...].astype(BF16), order[...], 1, 1)
    block_s[...] = jnp.zeros_like(block_s)
    point = w_point[...].astype(F32)
    for r in range(2):
        for j in range(6):
            block_s[pl.ds(12 + r * 6 + j, 1), :] = point[r:r + 1, j * TAKE:(j + 1) * TAKE]
    for x in range(NX):
        block_s[:9, :] = parted[:9, x * TAKE:(x + 1) * TAKE]
        block = block_s[...].astype(BF16)
        for z in range(NZ):
            out[z * NX + x] = block


def share_kernel(line, order, conv_share, point_share, rows_s, sum_s):
    me = lax.axis_index("x")
    rows_s[...] = jnp.zeros_like(rows_s)
    for x in range(NX):
        total = line[x].astype(F32)
        for z in range(1, NZ):
            total = total + line[z * NX + x].astype(F32)
        sum_s[...] = total
        rows_s[:9, x * TAKE:(x + 1) * TAKE] = sum_s[:9, :]
    total = line[me].astype(F32)
    for z in range(1, NZ):
        total = total + line[z * NX + me].astype(F32)
    sum_s[...] = total
    for r in range(2):
        for j in range(6):
            point_share[pl.ds(r, 1), j * TAKE:(j + 1) * TAKE] = sum_s[pl.ds(12 + r * 6 + j, 1), :]
    rows = rows_s[...]
    high = rows.astype(BF16)
    low = (rows - high.astype(F32)).astype(BF16)
    joined = dot(high, order[...], 1, 0) + dot(low, order[...], 1, 0)
    for t in range(3):
        for r in range(3):
            conv_share[r, pl.ds(t, 1), :] = joined[t * 3 + r:t * 3 + r + 1, :]


def slope_kernel(tokens, slope):
    for k in range(4):
        at = slice(k * 64, (k + 1) * 64)
        slope[at, :] = gelu_slope(tokens[at, :].astype(F32))


def add_kernel(mine, others, out):
    out[...] = (mine[...].astype(F32) + others[0].astype(F32)).astype(BF16)


def out_kernel(tokens, cotangent, slope, own, from_left, from_right, out_right, act_left, output, grad_tokens):
    for k in range(4):
        at = slice(k * 64, (k + 1) * 64)
        output[at, :] = (
            tokens[at, :].astype(F32) + own[0, at, :].astype(F32)
            + from_right[1, at, :].astype(F32) + out_right[at, :].astype(F32)
        ).astype(BF16)
        grad_act = own[1, at, :].astype(F32) + from_left[1, at, :].astype(F32) + act_left[at, :].astype(F32)
        grad_tokens[at, :] = (cotangent[at, :].astype(F32) + grad_act * slope[at, :]).astype(BF16)


def spread_kernel(line, conv_order, point_order, out, block_s, mine_s, all_s):
    me = lax.axis_index("x")
    for q in range(32):
        all_s[q * 24:(q + 1) * 24, :] = line[q].astype(F32)
    for z in range(NZ):
        mine_s[z * 24:(z + 1) * 24, :] = line[z * NX + me].astype(F32)
    for g in range(2):
        rows = dot(conv_order[...], all_s[g * 384:(g + 1) * 384, :].astype(BF16), 1, 0).astype(BF16)
        for t in range(3):
            block_s[t * 96 + g * 48:t * 96 + g * 48 + 48, :] = rows[t * 48:(t + 1) * 48]
    block_s[288:, :] = dot(point_order[...], mine_s[...].astype(BF16), 1, 0).astype(BF16)
    for p in range(8):
        out[p] = block_s[...]


def line_kernel(slab, conv_order, point_order, out, block_s, all_s):
    me = lax.axis_index("x")
    total = slab[0].astype(F32)
    for p in range(1, 8):
        total = total + slab[p].astype(F32)
    block_s[...] = total.astype(BF16)
    for g in range(2):
        rows = dot(conv_order[:, :48], block_s[g * 48:g * 48 + 48, :], 1, 0)
        for t in (1, 2):
            rows = rows + dot(
                conv_order[:, t * 48:(t + 1) * 48], block_s[t * 96 + g * 48:t * 96 + g * 48 + 48, :], 1, 0
            )
        for q in range(16):
            all_s[g * 16 + q] = rows[q * 24:(q + 1) * 24]
    rows = dot(point_order[...], block_s[288:, :], 1, 0)
    for z in range(NZ):
        all_s[z * NX + me] += rows[z * 24:(z + 1) * 24]
    for q in range(32):
        out[q] = all_s[q].astype(BF16)


def weights_kernel(slab, to_d, to_h, conv_w, point_w, rows_s, point_s):
    for g in range(2):
        for p in range(8):
            for t in range(3):
                at = t * 96 + g * 48
                rows_s[p * 48:(p + 1) * 48, t * TAKE:(t + 1) * TAKE] = slab[p, at:at + 48, :]
        conv_w[g * 384:(g + 1) * 384, :] = dot(to_d[...], rows_s[...], 1, 0).astype(BF16)
    for p in range(8):
        for j in range(6):
            at = 288 + j * 16
            point_s[p * 16:(p + 1) * 16, j * TAKE:(j + 1) * TAKE] = slab[p, at:at + 16, :]
    point_w[...] = dot(to_h[...], point_s[...], 1, 0).astype(BF16)


def middle_kernel(
    act0, act1, act2, act3, ct0, ct1, ct2, ct3, conv_w_far, point_w_far, from_d_far, from_h_far,
    grads_far, own_far, out_mid_far, act_mid_far, to_right_far, to_left_far,
    acts, cts, conv_w, point_w, from_d, from_h, grads, own, mids, to_right, to_left,
    inner_act, spread_grad, taps_s, grad_s, conv_g, in_sems, out_sems,
):
    me = lax.axis_index("x")
    place = [lax.rem(me + r, NX) for r in range(NX)]
    keep_before = [(p != 0).astype(F32) for p in place]
    keep_after = [(p != NX - 1).astype(F32) for p in place]
    copies = fetch(
        (conv_w_far, act0, act1, act2, act3, point_w_far, ct0, ct1, ct2, ct3, from_d_far, from_h_far),
        (conv_w, *[acts.at[r] for r in range(NX)], point_w, *[cts.at[r] for r in range(NX)], from_d, from_h),
        in_sems,
    )
    copies[0].wait()
    for r in range(NX):
        copies[1 + r].wait()
        taps_s[r] = dot(acts[r], conv_w[...], 1, 0)
    copies[5].wait()
    for r in range(NX):
        copies[6 + r].wait()
        grad_pre = dot(cts[r], point_w[...], 1, 1)
        conv_out = (
            taps_s[r, :, TAKE:2 * TAKE]
            + taps_s[(r - 1) % NX, :, :TAKE] * keep_before[r]
            + taps_s[(r + 1) % NX, :, 2 * TAKE:] * keep_after[r]
        )
        t = tanh_of(conv_out)
        cdf = 0.5 * (1.0 + t)
        inner_act[r] = (conv_out * cdf).astype(BF16)
        slope = cdf + (0.5 * conv_out) * (
            (1.0 - t * t) * (SCALE * (1.0 + 3.0 * CUBIC * (conv_out * conv_out)))
        )
        grad_s[r] = (grad_pre * slope).astype(BF16)
    for r in range(NX):
        spread_grad[r, :, :TAKE] = grad_s[(r + 1) % NX] * keep_after[r].astype(BF16)
        spread_grad[r, :, TAKE:2 * TAKE] = grad_s[r]
        spread_grad[r, :, 2 * TAKE:] = grad_s[(r - 1) % NX] * keep_before[r].astype(BF16)

    def out_part(r):
        return dot(inner_act[r], point_w[...], 1, 0).astype(BF16)

    def act_part(r):
        return dot(spread_grad[r], conv_w[...], 1, 1).astype(BF16)

    to_right[0], to_right[1] = out_part(2), act_part(1)
    sent = fetch((to_right,), (to_right_far,), out_sems)
    to_left[0], to_left[1] = act_part(2), out_part(3)
    sent += fetch((to_left,), (to_left_far,), out_sems, 1)

    for t in range(3):
        at = slice(t * TAKE, (t + 1) * TAKE)
        total = dot(spread_grad[0, :, at], acts[0], 0, 0)
        for r in range(1, NX):
            total = total + dot(spread_grad[r, :, at], acts[r], 0, 0)
        conv_g[:, at] = total.T.astype(BF16)
    copies[10].wait()
    copies[11].wait()
    for g in range(2):
        rows = dot(from_d[...], conv_g[g * 384:(g + 1) * 384, :], 1, 0).astype(BF16)
        for p in range(8):
            for t in range(3):
                grads[p, t * 96 + g * 48:t * 96 + g * 48 + 48, :] = rows[
                    p * 48:(p + 1) * 48, t * TAKE:(t + 1) * TAKE
                ]
    total = dot(inner_act[0], cts[0], 0, 0)
    for r in range(1, NX):
        total = total + dot(inner_act[r], cts[r], 0, 0)
    rows = dot(from_h[...], total.astype(BF16), 1, 0).astype(BF16)
    for p in range(8):
        for j in range(6):
            grads[p, 288 + j * 16:304 + j * 16, :] = rows[
                p * 16:(p + 1) * 16, j * TAKE:(j + 1) * TAKE
            ]
    sent += fetch((grads,), (grads_far,), out_sems, 2)
    own[0], own[1] = out_part(0), act_part(0)
    sent += fetch((own,), (own_far,), out_sems, 3)
    mids[0], mids[1] = out_part(1), act_part(3)
    sent += fetch((mids.at[0], mids.at[1]), (out_mid_far, act_mid_far), out_sems, 4)
    for copy in sent:
        copy.wait()


def shards(tokens, cotangent, w_conv, w_point):
    def constant(matrix):
        return jnp.asarray(matrix, BF16)

    columns, conv_rows, point_rows = column_order(), conv_rows_order(), point_rows_order()
    channels, inner = channel_order(), inner_order()

    own = kernel_call(
        own_kernel, shape(32, 24, TAKE),
        scratch=[
            pltpu.VMEM((16, INNER), F32), pltpu.VMEM((24, TAKE), F32),
            pltpu.VMEM((3, 3, INNER), BF16), pltpu.VMEM((2, D), BF16), pltpu.VMEM((INNER, INNER), BF16),
            pltpu.SemaphoreType.DMA((3,)),
        ],
        moved=2**19, far=3, limit=60,
    )(w_conv, w_point, constant(columns))
    line = lax.all_to_all(own, SHEET, 0, 0)
    act, ct = [None] * NX, [None] * NX
    act[0] = gelu_tanh(tokens[0].astype(F32)).astype(BF16)
    ct[0] = cotangent[0]
    act[3], act[1] = step_along_x(act[0], 1), step_along_x(act[0], -1)
    ct[3], ct[1] = step_along_x(ct[0], 1), step_along_x(ct[0], -1)
    line, act[1], act[3], ct[1], ct[3] = lax.optimization_barrier((line, act[1], act[3], ct[1], ct[3]))
    act[2] = step_along_x(act[3], 1)
    ct[2] = step_along_x(ct[1], -1)

    blocks = kernel_call(
        spread_kernel, shape(8, 384, TAKE),
        scratch=[pltpu.VMEM((384, TAKE), BF16), pltpu.VMEM((192, TAKE), F32), pltpu.VMEM((D, TAKE), F32)],
        flops=10**8, moved=2**20,
    )(line, constant(conv_rows), constant(point_rows))
    slab = lax.all_to_all(blocks, SLAB, 0, 0)
    conv_w, point_w = kernel_call(
        weights_kernel,
        [shape(D, 3 * TAKE), shape(TAKE, D)],
        scratch=[pltpu.VMEM((384, 3 * TAKE), BF16), pltpu.VMEM((TAKE, D), BF16)],
        flops=10**9,
        moved=3 * 2**20,
    )(slab, constant(channels), constant(inner))

    blocks = (2, ROWS, D)
    grads, own, out_mid, act_mid, to_right, to_left = kernel_call(
        middle_kernel,
        [
            shape(8, 384, TAKE), shape(*blocks), shape(ROWS, D), shape(ROWS, D), shape(*blocks), shape(*blocks),
        ],
        scratch=[
            pltpu.VMEM((NX, ROWS, D), BF16), pltpu.VMEM((NX, ROWS, D), BF16),
            pltpu.VMEM((D, 3 * TAKE), BF16), pltpu.VMEM((TAKE, D), BF16),
            pltpu.VMEM((384, 384), BF16), pltpu.VMEM((TAKE, TAKE), BF16),
            pltpu.VMEM((8, 384, TAKE), BF16),
            *[pltpu.VMEM(blocks, BF16)] * 4,
            pltpu.VMEM((NX, ROWS, TAKE), BF16),
            pltpu.VMEM((NX, ROWS, 3 * TAKE), BF16),
            pltpu.VMEM((NX, ROWS, 3 * TAKE), F32),
            pltpu.VMEM((NX, ROWS, TAKE), BF16),
            pltpu.VMEM((D, 3 * TAKE), BF16),
            pltpu.SemaphoreType.DMA((12,)),
            pltpu.SemaphoreType.DMA((6,)),
        ],
        flops=5 * 10**9,
        moved=12 * 2**20,
        limit=60,
        far=12,
        far_out=True,
    )(*act, *ct, conv_w, point_w, constant(channels.T), constant(inner.T))
    slab_g = lax.all_to_all(grads, SLAB, 0, 0)

    from_left, from_right = step_along_x(to_right, 1), step_along_x(to_left, -1)
    add = kernel_call(add_kernel, shape(ROWS, D), moved=2**20)
    out_right = step_along_x(add(out_mid, from_left), 1)
    act_left = step_along_x(add(act_mid, from_right), -1)
    slope = kernel_call(slope_kernel, shape(ROWS, D, dtype=F32), flops=10**7, moved=2**20)(tokens[0])
    output, grad_tokens = kernel_call(
        out_kernel, [shape(ROWS, D), shape(ROWS, D)], flops=10**7, moved=4 * 2**20
    )(tokens[0], ct[0], slope, own, from_left, from_right, out_right, act_left)

    line_g = kernel_call(
        line_kernel, shape(32, 24, TAKE),
        scratch=[pltpu.VMEM((384, TAKE), BF16), pltpu.VMEM((32, 24, TAKE), F32)],
        flops=10**8, moved=2**20,
    )(slab_g, constant(conv_rows.T), constant(point_rows.T))
    line_g = lax.all_to_all(line_g, SHEET, 0, 0)
    line_g, output, grad_tokens = lax.optimization_barrier((line_g, output, grad_tokens))
    conv_share, point_share = kernel_call(
        share_kernel,
        [shape(3, 3, INNER, dtype=F32), shape(2, D, dtype=F32)],
        scratch=[pltpu.VMEM((16, INNER), F32), pltpu.VMEM((24, TAKE), F32)],
        moved=2**18,
    )(line_g, constant(columns))
    return (output[None], grad_tokens[None], conv_share, point_share)


def solution(mesh):
    fine = Mesh(mesh.devices.reshape(NZ, NYH, NX, NYL, NC), AXES)
    dp, seq = ("z", "yh"), ("x", "yl", "core")
    rows = P(dp, seq, None)
    return jax.shard_map(
        shards,
        mesh=fine,
        in_specs=(rows, rows, P(None, AXES, None), P(AXES, None)),
        out_specs=(rows, rows, P(AXES, None, None), P(AXES, None)),
        check_vma=False,
    )
```

```python
import numpy as np
import jax
import jax.numpy as jnp
from jax import lax
from jax.experimental import pallas as pl
from jax.experimental.pallas import tpu as pltpu
from jax.sharding import Mesh, PartitionSpec as P

NZ, NYH, NX, NYL, NC = 8, 2, 4, 2, 2
AXES = ("z", "yh", "x", "yl", "core")
SLAB = ("yh", "yl", "core")
SHEET = ("z", "x")
ROWS, D, INNER, TAKE = 256, 768, 512, 128
BF16 = jnp.bfloat16
F32 = jnp.float32
SCALE = 0.7978845608028654
CUBIC = 0.044715


def one_hot_rows(source):
    source = np.asarray(source).reshape(-1)
    matrix = np.zeros((source.size, source.size), np.float32)
    matrix[np.arange(source.size), source] = 1.0
    return matrix


def column_order():
    return one_hot_rows([
        64 * z + 32 * yh + 8 * x + low
        for x in range(NX) for z in range(NZ) for yh in range(NYH) for low in range(8)
    ])


def conv_rows_order():
    matrix = np.zeros((144, 384), np.float32)
    for t, q, r in np.ndindex(3, 16, 3):
        matrix[t * 48 + q * 3 + r, q * 24 + t * 3 + r] = 1.0
    return matrix


def point_rows_order():
    matrix = np.zeros((96, 192), np.float32)
    for j, z, r in np.ndindex(6, NZ, 2):
        matrix[j * 16 + z * 2 + r, z * 24 + 12 + r * 6 + j] = 1.0
    return matrix


def channel_order():
    return one_hot_rows([
        ((yh * 2 + yl) * 2 + core) * 48 + z * 12 + x * 3 + r
        for z in range(4) for yh in range(NYH) for x in range(NX)
        for yl in range(NYL) for core in range(NC) for r in range(3)
    ])


def inner_order():
    return one_hot_rows([p * 16 + z * 2 + r for z in range(NZ) for p in range(8) for r in range(2)])


def step_along_x(value, step):
    return lax.ppermute(value, "x", [(i, (i + step) % NX) for i in range(NX)])


def tanh_of(values):
    return jnp.tanh(SCALE * (values + CUBIC * (values * values * values)))


def gelu_tanh(values):
    return values * (0.5 * (1.0 + tanh_of(values)))


def gelu_slope(values):
    t = tanh_of(values)
    return 0.5 * (1.0 + t) + (0.5 * values) * ((1.0 - t * t) * (SCALE * (1.0 + 3.0 * CUBIC * (values * values))))


def dot(left, right, left_dim, right_dim):
    return lax.dot_general(
        left, right, (((left_dim,), (right_dim,)), ((), ())), preferred_element_type=F32
    )


def kernel_call(body, out_shapes, scratch=(), flops=0, moved=0, limit=8, far=0, far_out=False):
    many = isinstance(out_shapes, (list, tuple))
    vmem, hbm = pl.BlockSpec(memory_space=pltpu.VMEM), pl.BlockSpec(memory_space=pltpu.HBM)
    out_spec = hbm if far_out else vmem

    def call(*operands):
        return pl.pallas_call(
            body,
            out_shape=out_shapes,
            in_specs=[vmem] * (len(operands) - far) + [hbm] * far,
            out_specs=[out_spec] * len(out_shapes) if many else out_spec,
            scratch_shapes=list(scratch),
            compiler_params=pltpu.CompilerParams(vmem_limit_bytes=limit * 2**20),
            cost_estimate=pl.CostEstimate(flops=flops, bytes_accessed=moved, transcendentals=0),
        )(*operands)

    return call


def shape(*dims, dtype=BF16):
    return jax.ShapeDtypeStruct(dims, dtype)


def fetch(sources, targets, sems, first=0):
    copies = [
        pltpu.make_async_copy(source, target, sems.at[first + k])
        for k, (source, target) in enumerate(zip(sources, targets))
    ]
    for copy in copies:
        copy.start()
    return copies


def front_kernel(
    w_conv_far, w_point_far, order_far, tokens_far,
    out_far, act_far,
    rows_s, block_s, w_conv, w_point, order, tokens, act, own_s, in_sems, out_sems,
):
    copies = fetch(
        (tokens_far.at[0], w_conv_far, w_point_far, order_far),
        (tokens, w_conv, w_point, order),
        in_sems,
    )
    for copy in copies[1:]:
        copy.wait()
    rows_s[...] = jnp.zeros_like(rows_s)
    for t in range(3):
        rows_s[t * 3:(t + 1) * 3, :] = w_conv[t].astype(F32)
    parted = dot(rows_s[...].astype(BF16), order[...], 1, 1)
    block_s[...] = jnp.zeros_like(block_s)
    point = w_point[...].astype(F32)
    for r in range(2):
        for j in range(6):
            block_s[pl.ds(12 + r * 6 + j, 1), :] = point[r:r + 1, j * TAKE:(j + 1) * TAKE]
    for x in range(NX):
        block_s[:9, :] = parted[:9, x * TAKE:(x + 1) * TAKE]
        block = block_s[...].astype(BF16)
        for z in range(NZ):
            own_s[z * NX + x] = block
    sent = fetch((own_s,), (out_far,), out_sems)
    copies[0].wait()
    for k in range(4):
        at = slice(k * 64, (k + 1) * 64)
        act[at, :] = gelu_tanh(tokens[at, :].astype(F32)).astype(BF16)
    sent += fetch((act,), (act_far,), out_sems, 1)
    for copy in sent:
        copy.wait()


def share_kernel(line, order, conv_share, point_share, rows_s, sum_s):
    me = lax.axis_index("x")
    rows_s[...] = jnp.zeros_like(rows_s)
    for x in range(NX):
        total = line[x].astype(F32)
        for z in range(1, NZ):
            total = total + line[z * NX + x].astype(F32)
        sum_s[...] = total
        rows_s[:9, x * TAKE:(x + 1) * TAKE] = sum_s[:9, :]
    total = line[me].astype(F32)
    for z in range(1, NZ):
        total = total + line[z * NX + me].astype(F32)
    sum_s[...] = total
    for r in range(2):
        for j in range(6):
            point_share[pl.ds(r, 1), j * TAKE:(j + 1) * TAKE] = sum_s[pl.ds(12 + r * 6 + j, 1), :]
    rows = rows_s[...]
    high = rows.astype(BF16)
    low = (rows - high.astype(F32)).astype(BF16)
    joined = dot(high, order[...], 1, 0) + dot(low, order[...], 1, 0)
    for t in range(3):
        for r in range(3):
            conv_share[r, pl.ds(t, 1), :] = joined[t * 3 + r:t * 3 + r + 1, :]


def slope_kernel(tokens, slope):
    for k in range(4):
        at = slice(k * 64, (k + 1) * 64)
        slope[at, :] = gelu_slope(tokens[at, :].astype(F32))


def add_kernel(mine, other, out):
    out[...] = (mine[...].astype(F32) + other[...].astype(F32)).astype(BF16)


def out_kernel(
    tokens, cotangent, slope, own, out_left, out_right, act_left, act_right, output, grad_tokens
):
    for k in range(4):
        at = slice(k * 64, (k + 1) * 64)
        output[at, :] = (
            tokens[at, :].astype(F32) + own[0, at, :].astype(F32)
            + out_left[at, :].astype(F32) + out_right[at, :].astype(F32)
        ).astype(BF16)
        grad_act = own[1, at, :].astype(F32) + act_right[at, :].astype(F32) + act_left[at, :].astype(F32)
        grad_tokens[at, :] = (cotangent[at, :].astype(F32) + grad_act * slope[at, :]).astype(BF16)


def spread_kernel(line, conv_order, point_order, out, block_s, mine_s, all_s):
    me = lax.axis_index("x")
    for q in range(32):
        all_s[q * 24:(q + 1) * 24, :] = line[q].astype(F32)
    for z in range(NZ):
        mine_s[z * 24:(z + 1) * 24, :] = line[z * NX + me].astype(F32)
    for g in range(2):
        rows = dot(conv_order[...], all_s[g * 384:(g + 1) * 384, :].astype(BF16), 1, 0).astype(BF16)
        for t in range(3):
            block_s[t * 96 + g * 48:t * 96 + g * 48 + 48, :] = rows[t * 48:(t + 1) * 48]
    block_s[288:, :] = dot(point_order[...], mine_s[...].astype(BF16), 1, 0).astype(BF16)
    for p in range(8):
        out[p] = block_s[...]


def line_kernel(slab, conv_order, point_order, out, block_s, all_s):
    me = lax.axis_index("x")
    total = slab[0].astype(F32)
    for p in range(1, 8):
        total = total + slab[p].astype(F32)
    block_s[...] = total.astype(BF16)
    for g in range(2):
        rows = dot(conv_order[:, :48], block_s[g * 48:g * 48 + 48, :], 1, 0)
        for t in (1, 2):
            rows = rows + dot(
                conv_order[:, t * 48:(t + 1) * 48], block_s[t * 96 + g * 48:t * 96 + g * 48 + 48, :], 1, 0
            )
        for q in range(16):
            all_s[g * 16 + q] = rows[q * 24:(q + 1) * 24]
    rows = dot(point_order[...], block_s[288:, :], 1, 0)
    for z in range(NZ):
        all_s[z * NX + me] += rows[z * 24:(z + 1) * 24]
    for q in range(32):
        out[q] = all_s[q].astype(BF16)


def middle_kernel(
    slab_far, to_d_far, to_h_far, from_d_far, from_h_far, *refs,
):
    parts_far, refs = refs[:10], refs[10:]
    grads_far, own_far, out1_far, act3_far, out2_far, act2_far, out3_far, act1_far = refs[:8]
    (
        slab, to_d, to_h, acts, cts, conv_w, point_w, from_d, from_h, rows_s, point_s, grads, sends,
        inner_act, spread_grad, taps_s, grad_s, conv_g, in_sems, out_sems,
    ) = refs[8:]
    me = lax.axis_index("x")
    place = [lax.rem(me + r, NX) for r in range(NX)]
    keep_before = [(p != 0).astype(F32) for p in place]
    keep_after = [(p != NX - 1).astype(F32) for p in place]
    top, low = slice(0, ROWS // 2), slice(ROWS // 2, ROWS)
    places = [
        full.at[r, at] for full in (acts, cts)
        for r, at in ((0, slice(None)), (1, slice(None)), (3, slice(None)), (2, top), (2, low))
    ]
    copies = fetch(
        (slab_far, to_d_far, to_h_far, *parts_far, from_d_far, from_h_far),
        (slab, to_d, to_h, *places, from_d, from_h),
        in_sems,
    )
    for copy in copies[:3]:
        copy.wait()
    for g in range(2):
        for p in range(8):
            for t in range(3):
                at = t * 96 + g * 48
                rows_s[p * 48:(p + 1) * 48, t * TAKE:(t + 1) * TAKE] = slab[p, at:at + 48, :]
        conv_w[g * 384:(g + 1) * 384, :] = dot(to_d[...], rows_s[...], 1, 0).astype(BF16)
    for p in range(8):
        for j in range(6):
            at = 288 + j * 16
            point_s[p * 16:(p + 1) * 16, j * TAKE:(j + 1) * TAKE] = slab[p, at:at + 16, :]
    point_w[...] = dot(to_h[...], point_s[...], 1, 0).astype(BF16)
    for copy in copies[3:8]:
        copy.wait()
    for r in range(NX):
        taps_s[r] = dot(acts[r], conv_w[...], 1, 0)
    for copy in copies[8:13]:
        copy.wait()
    for r in range(NX):
        grad_pre = dot(cts[r], point_w[...], 1, 1)
        conv_out = (
            taps_s[r, :, TAKE:2 * TAKE]
            + taps_s[(r - 1) % NX, :, :TAKE] * keep_before[r]
            + taps_s[(r + 1) % NX, :, 2 * TAKE:] * keep_after[r]
        )
        t = tanh_of(conv_out)
        cdf = 0.5 * (1.0 + t)
        inner_act[r] = (conv_out * cdf).astype(BF16)
        slope = cdf + (0.5 * conv_out) * (
            (1.0 - t * t) * (SCALE * (1.0 + 3.0 * CUBIC * (conv_out * conv_out)))
        )
        grad_s[r] = (grad_pre * slope).astype(BF16)
    for r in range(NX):
        spread_grad[r, :, :TAKE] = grad_s[(r + 1) % NX] * keep_after[r].astype(BF16)
        spread_grad[r, :, TAKE:2 * TAKE] = grad_s[r]
        spread_grad[r, :, 2 * TAKE:] = grad_s[(r - 1) % NX] * keep_before[r].astype(BF16)

    def out_part(r):
        return dot(inner_act[r], point_w[...], 1, 0).astype(BF16)

    def act_part(r):
        return dot(spread_grad[r], conv_w[...], 1, 1).astype(BF16)

    sent = []

    def send(k, value, target):
        sends[k] = value
        sent.extend(fetch((sends.at[k],), (target,), out_sems, k))

    send(0, out_part(2), out2_far)
    send(1, act_part(2), act2_far)
    send(2, out_part(3), out3_far)
    send(3, act_part(1), act1_far)
    send(4, out_part(1), out1_far)
    send(5, act_part(3), act3_far)
    send(6, out_part(0), own_far.at[0])
    send(7, act_part(0), own_far.at[1])

    for t in range(3):
        at = slice(t * TAKE, (t + 1) * TAKE)
        total = dot(spread_grad[0, :, at], acts[0], 0, 0)
        for r in range(1, NX):
            total = total + dot(spread_grad[r, :, at], acts[r], 0, 0)
        conv_g[:, at] = total.T.astype(BF16)
    copies[13].wait()
    copies[14].wait()
    for g in range(2):
        rows = dot(from_d[...], conv_g[g * 384:(g + 1) * 384, :], 1, 0).astype(BF16)
        for p in range(8):
            for t in range(3):
                grads[p, t * 96 + g * 48:t * 96 + g * 48 + 48, :] = rows[
                    p * 48:(p + 1) * 48, t * TAKE:(t + 1) * TAKE
                ]
    total = dot(inner_act[0], cts[0], 0, 0)
    for r in range(1, NX):
        total = total + dot(inner_act[r], cts[r], 0, 0)
    rows = dot(from_h[...], total.astype(BF16), 1, 0).astype(BF16)
    for p in range(8):
        for j in range(6):
            grads[p, 288 + j * 16:304 + j * 16, :] = rows[
                p * 16:(p + 1) * 16, j * TAKE:(j + 1) * TAKE
            ]
    sent.extend(fetch((grads,), (grads_far,), out_sems, 8))
    for copy in sent:
        copy.wait()


def shards(tokens, cotangent, w_conv, w_point):
    def constant(matrix):
        return jnp.asarray(matrix, BF16)

    columns, conv_rows, point_rows = column_order(), conv_rows_order(), point_rows_order()
    channels, inner = channel_order(), inner_order()

    act, ct = [None] * NX, [None] * NX
    own, act[0] = kernel_call(
        front_kernel, [shape(32, 24, TAKE), shape(ROWS, D)],
        scratch=[
            pltpu.VMEM((16, INNER), F32), pltpu.VMEM((24, TAKE), F32),
            pltpu.VMEM((3, 3, INNER), BF16), pltpu.VMEM((2, D), BF16), pltpu.VMEM((INNER, INNER), BF16),
            pltpu.VMEM((ROWS, D), BF16), pltpu.VMEM((ROWS, D), BF16), pltpu.VMEM((32, 24, TAKE), BF16),
            pltpu.SemaphoreType.DMA((4,)), pltpu.SemaphoreType.DMA((2,)),
        ],
        flops=10**7, moved=2 * 2**20, far=4, far_out=True, limit=60,
    )(w_conv, w_point, constant(columns), tokens)
    line = lax.all_to_all(own, SHEET, 0, 0)
    ct[0] = cotangent[0]
    act[3], act[1] = step_along_x(act[0], 1), step_along_x(act[0], -1)
    ct[3], ct[1] = step_along_x(ct[0], 1), step_along_x(ct[0], -1)
    def far_block(blocks):
        top, low = blocks[3][:ROWS // 2], blocks[1][ROWS // 2:]
        return step_along_x(top, 1), step_along_x(low, -1)

    line, act[1], act[3], ct[1], ct[3] = lax.optimization_barrier((line, act[1], act[3], ct[1], ct[3]))
    act[2] = far_block(act)
    ct[2] = far_block(ct)
    blocks = kernel_call(
        spread_kernel, shape(8, 384, TAKE),
        scratch=[pltpu.VMEM((384, TAKE), BF16), pltpu.VMEM((192, TAKE), F32), pltpu.VMEM((D, TAKE), F32)],
        flops=2 * 10**10, moved=2**20,
    )(line, constant(conv_rows), constant(point_rows))
    slab = lax.all_to_all(blocks, SLAB, 0, 0)
    block = shape(ROWS, D)
    grads, own, out1, act3, out2, act2, out3, act1 = kernel_call(
        middle_kernel,
        [shape(8, 384, TAKE), shape(2, ROWS, D)] + [block] * 6,
        scratch=[
            pltpu.VMEM((8, 384, TAKE), BF16), pltpu.VMEM((384, 384), BF16), pltpu.VMEM((TAKE, TAKE), BF16),
            pltpu.VMEM((NX, ROWS, D), BF16), pltpu.VMEM((NX, ROWS, D), BF16),
            pltpu.VMEM((D, 3 * TAKE), BF16), pltpu.VMEM((TAKE, D), BF16),
            pltpu.VMEM((384, 384), BF16), pltpu.VMEM((TAKE, TAKE), BF16),
            pltpu.VMEM((384, 3 * TAKE), BF16), pltpu.VMEM((TAKE, D), BF16),
            pltpu.VMEM((8, 384, TAKE), BF16),
            pltpu.VMEM((8, ROWS, D), BF16),
            pltpu.VMEM((NX, ROWS, TAKE), BF16),
            pltpu.VMEM((NX, ROWS, 3 * TAKE), BF16),
            pltpu.VMEM((NX, ROWS, 3 * TAKE), F32),
            pltpu.VMEM((NX, ROWS, TAKE), BF16),
            pltpu.VMEM((D, 3 * TAKE), BF16),
            pltpu.SemaphoreType.DMA((15,)),
            pltpu.SemaphoreType.DMA((9,)),
        ],
        flops=5 * 10**9,
        moved=12 * 2**20,
        limit=60,
        far=15,
        far_out=True,
    )(
        slab, constant(channels), constant(inner), constant(channels.T), constant(inner.T),
        act[0], act[1], act[3], *act[2], ct[0], ct[1], ct[3], *ct[2],
    )
    slab_g = lax.all_to_all(grads, SLAB, 0, 0)

    out_far, act_far = step_along_x(out2, 1), step_along_x(act2, -1)
    out_left, act_right = step_along_x(out3, -1), step_along_x(act1, 1)
    line_g = kernel_call(
        line_kernel, shape(32, 24, TAKE),
        scratch=[pltpu.VMEM((384, TAKE), BF16), pltpu.VMEM((32, 24, TAKE), F32)],
        flops=10**8, moved=2**20,
    )(slab_g, constant(conv_rows.T), constant(point_rows.T))
    add = kernel_call(add_kernel, block, moved=2**20)
    out_right = step_along_x(add(out1, out_far), 1)
    act_left = step_along_x(add(act3, act_far), -1)
    slope = kernel_call(slope_kernel, shape(ROWS, D, dtype=F32), flops=10**7, moved=2**20)(tokens[0])
    output, grad_tokens = kernel_call(
        out_kernel, [shape(ROWS, D), shape(ROWS, D)], flops=10**7, moved=4 * 2**20
    )(tokens[0], cotangent[0], slope, own, out_left, out_right, act_left, act_right)

    line_g = lax.all_to_all(line_g, SHEET, 0, 0)
    line_g, output, grad_tokens = lax.optimization_barrier((line_g, output, grad_tokens))
    conv_share, point_share = kernel_call(
        share_kernel,
        [shape(3, 3, INNER, dtype=F32), shape(2, D, dtype=F32)],
        scratch=[pltpu.VMEM((16, INNER), F32), pltpu.VMEM((24, TAKE), F32)],
        moved=2**18,
    )(line_g, constant(columns))
    return (output[None], grad_tokens[None], conv_share, point_share)


def solution(mesh):
    fine = Mesh(mesh.devices.reshape(NZ, NYH, NX, NYL, NC), AXES)
    dp, seq = ("z", "yh"), ("x", "yl", "core")
    rows = P(dp, seq, None)
    return jax.shard_map(
        shards,
        mesh=fine,
        in_specs=(rows, rows, P(None, AXES, None), P(AXES, None)),
        out_specs=(rows, rows, P(AXES, None, None), P(AXES, None)),
        check_vma=False,
    )
```

```python
import numpy as np
import jax
import jax.numpy as jnp
from jax import lax
from jax.experimental import pallas as pl
from jax.experimental.pallas import tpu as pltpu
from jax.sharding import Mesh, PartitionSpec as P

NZ, NYH, NX, NYL, NC = 8, 2, 4, 2, 2
AXES = ("z", "yh", "x", "yl", "core")
SLAB = ("yh", "yl", "core")
SHEET = ("z", "x")
ROWS, D, INNER, TAKE = 256, 768, 512, 128
BF16 = jnp.bfloat16
F32 = jnp.float32
SCALE = 0.7978845608028654
CUBIC = 0.044715


def one_hot_rows(source):
    source = np.asarray(source).reshape(-1)
    matrix = np.zeros((source.size, source.size), np.float32)
    matrix[np.arange(source.size), source] = 1.0
    return matrix


def column_order():
    return one_hot_rows([
        64 * z + 32 * yh + 8 * x + low
        for x in range(NX) for z in range(NZ) for yh in range(NYH) for low in range(8)
    ])


def conv_rows_order():
    matrix = np.zeros((144, 384), np.float32)
    for t, q, r in np.ndindex(3, 16, 3):
        matrix[t * 48 + q * 3 + r, q * 24 + t * 3 + r] = 1.0
    return matrix


def point_rows_order():
    matrix = np.zeros((96, 192), np.float32)
    for j, z, r in np.ndindex(6, NZ, 2):
        matrix[j * 16 + z * 2 + r, z * 24 + 12 + r * 6 + j] = 1.0
    return matrix


def channel_order():
    return one_hot_rows([
        ((yh * 2 + yl) * 2 + core) * 48 + z * 12 + x * 3 + r
        for z in range(4) for yh in range(NYH) for x in range(NX)
        for yl in range(NYL) for core in range(NC) for r in range(3)
    ])


def inner_order():
    return one_hot_rows([p * 16 + z * 2 + r for z in range(NZ) for p in range(8) for r in range(2)])


def step_along_x(value, step):
    return lax.ppermute(value, "x", [(i, (i + step) % NX) for i in range(NX)])


def tanh_of(values):
    return jnp.tanh(SCALE * (values + CUBIC * (values * values * values)))


def gelu_tanh(values):
    return values * (0.5 * (1.0 + tanh_of(values)))


def gelu_slope(values):
    t = tanh_of(values)
    return 0.5 * (1.0 + t) + (0.5 * values) * ((1.0 - t * t) * (SCALE * (1.0 + 3.0 * CUBIC * (values * values))))


def dot(left, right, left_dim, right_dim):
    return lax.dot_general(
        left, right, (((left_dim,), (right_dim,)), ((), ())), preferred_element_type=F32
    )


def kernel_call(body, out_shapes, scratch=(), flops=0, moved=0, limit=8, far=0, far_out=False):
    many = isinstance(out_shapes, (list, tuple))
    vmem, hbm = pl.BlockSpec(memory_space=pltpu.VMEM), pl.BlockSpec(memory_space=pltpu.HBM)
    out_spec = hbm if far_out else vmem

    def call(*operands):
        return pl.pallas_call(
            body,
            out_shape=out_shapes,
            in_specs=[vmem] * (len(operands) - far) + [hbm] * far,
            out_specs=[out_spec] * len(out_shapes) if many else out_spec,
            scratch_shapes=list(scratch),
            compiler_params=pltpu.CompilerParams(vmem_limit_bytes=limit * 2**20),
            cost_estimate=pl.CostEstimate(flops=flops, bytes_accessed=moved, transcendentals=0),
        )(*operands)

    return call


def shape(*dims, dtype=BF16):
    return jax.ShapeDtypeStruct(dims, dtype)


def fetch(sources, targets, sems, first=0):
    copies = [
        pltpu.make_async_copy(source, target, sems.at[first + k])
        for k, (source, target) in enumerate(zip(sources, targets))
    ]
    for copy in copies:
        copy.start()
    return copies


def front_kernel(
    w_conv_far, w_point_far, order_far, tokens_far,
    out_far, act_far,
    rows_s, block_s, w_conv, w_point, order, tokens, act, own_s, in_sems, out_sems,
):
    copies = fetch(
        (tokens_far.at[0], w_conv_far, w_point_far, order_far),
        (tokens, w_conv, w_point, order),
        in_sems,
    )
    for copy in copies[1:]:
        copy.wait()
    rows_s[...] = jnp.zeros_like(rows_s)
    for t in range(3):
        rows_s[t * 3:(t + 1) * 3, :] = w_conv[t].astype(F32)
    parted = dot(rows_s[...].astype(BF16), order[...], 1, 1)
    block_s[...] = jnp.zeros_like(block_s)
    point = w_point[...].astype(F32)
    for r in range(2):
        for j in range(6):
            block_s[pl.ds(12 + r * 6 + j, 1), :] = point[r:r + 1, j * TAKE:(j + 1) * TAKE]
    for x in range(NX):
        block_s[:9, :] = parted[:9, x * TAKE:(x + 1) * TAKE]
        block = block_s[...].astype(BF16)
        for z in range(NZ):
            own_s[z * NX + x] = block
    sent = fetch((own_s,), (out_far,), out_sems)
    copies[0].wait()
    for k in range(4):
        at = slice(k * 64, (k + 1) * 64)
        act[at, :] = gelu_tanh(tokens[at, :].astype(F32)).astype(BF16)
    sent += fetch((act,), (act_far,), out_sems, 1)
    for copy in sent:
        copy.wait()


def share_kernel(line, order, conv_share, point_share, rows_s, sum_s):
    me = lax.axis_index("x")
    rows_s[...] = jnp.zeros_like(rows_s)
    for x in range(NX):
        total = line[x].astype(F32)
        for z in range(1, NZ):
            total = total + line[z * NX + x].astype(F32)
        sum_s[...] = total
        rows_s[:9, x * TAKE:(x + 1) * TAKE] = sum_s[:9, :]
    total = line[me].astype(F32)
    for z in range(1, NZ):
        total = total + line[z * NX + me].astype(F32)
    sum_s[...] = total
    for r in range(2):
        for j in range(6):
            point_share[pl.ds(r, 1), j * TAKE:(j + 1) * TAKE] = sum_s[pl.ds(12 + r * 6 + j, 1), :]
    rows = rows_s[...]
    high = rows.astype(BF16)
    low = (rows - high.astype(F32)).astype(BF16)
    joined = dot(high, order[...], 1, 0) + dot(low, order[...], 1, 0)
    for t in range(3):
        for r in range(3):
            conv_share[r, pl.ds(t, 1), :] = joined[t * 3 + r:t * 3 + r + 1, :]


def slope_kernel(tokens, slope):
    for k in range(4):
        at = slice(k * 64, (k + 1) * 64)
        slope[at, :] = gelu_slope(tokens[at, :].astype(F32))


def add_kernel(mine, other, out):
    out[...] = (mine[...].astype(F32) + other[...].astype(F32)).astype(BF16)


def out_kernel(
    tokens, cotangent, slope, own, out_left, out_right, act_left, act_right, output, grad_tokens
):
    for k in range(4):
        at = slice(k * 64, (k + 1) * 64)
        output[at, :] = (
            tokens[at, :].astype(F32) + own[0, at, :].astype(F32)
            + out_left[at, :].astype(F32) + out_right[at, :].astype(F32)
        ).astype(BF16)
        grad_act = own[1, at, :].astype(F32) + act_right[at, :].astype(F32) + act_left[at, :].astype(F32)
        grad_tokens[at, :] = (cotangent[at, :].astype(F32) + grad_act * slope[at, :]).astype(BF16)


def spread_kernel(line, conv_order, point_order, out, block_s, mine_s, all_s):
    me = lax.axis_index("x")
    for q in range(32):
        all_s[q * 24:(q + 1) * 24, :] = line[q].astype(F32)
    for z in range(NZ):
        mine_s[z * 24:(z + 1) * 24, :] = line[z * NX + me].astype(F32)
    for g in range(2):
        rows = dot(conv_order[...], all_s[g * 384:(g + 1) * 384, :].astype(BF16), 1, 0).astype(BF16)
        for t in range(3):
            block_s[t * 96 + g * 48:t * 96 + g * 48 + 48, :] = rows[t * 48:(t + 1) * 48]
    block_s[288:, :] = dot(point_order[...], mine_s[...].astype(BF16), 1, 0).astype(BF16)
    for p in range(8):
        out[p] = block_s[...]


def line_kernel(slab, conv_order, point_order, out, block_s, all_s):
    me = lax.axis_index("x")
    total = slab[0].astype(F32)
    for p in range(1, 8):
        total = total + slab[p].astype(F32)
    block_s[...] = total.astype(BF16)
    for g in range(2):
        rows = dot(conv_order[:, :48], block_s[g * 48:g * 48 + 48, :], 1, 0)
        for t in (1, 2):
            rows = rows + dot(
                conv_order[:, t * 48:(t + 1) * 48], block_s[t * 96 + g * 48:t * 96 + g * 48 + 48, :], 1, 0
            )
        for q in range(16):
            all_s[g * 16 + q] = rows[q * 24:(q + 1) * 24]
    rows = dot(point_order[...], block_s[288:, :], 1, 0)
    for z in range(NZ):
        all_s[z * NX + me] += rows[z * 24:(z + 1) * 24]
    for q in range(32):
        out[q] = all_s[q].astype(BF16)


def middle_kernel(
    slab_far, to_d_far, to_h_far, from_d_far, from_h_far, *refs,
):
    parts_far, refs = refs[:10], refs[10:]
    grads_far, own_far, out1_far, act3_far, out2_far, act2_far, out3_far, act1_far = refs[:8]
    (
        slab, to_d, to_h, acts, cts, conv_w, point_w, from_d, from_h, rows_s, point_s, grads, sends,
        inner_act, spread_grad, taps_s, grad_s, conv_g, in_sems, out_sems,
    ) = refs[8:]
    me = lax.axis_index("x")
    place = [lax.rem(me + r, NX) for r in range(NX)]
    keep_before = [(p != 0).astype(F32) for p in place]
    keep_after = [(p != NX - 1).astype(F32) for p in place]
    top, low = slice(0, ROWS // 2), slice(ROWS // 2, ROWS)
    places = [
        full.at[r, at] for full in (acts, cts)
        for r, at in ((0, slice(None)), (1, slice(None)), (3, slice(None)), (2, top), (2, low))
    ]
    copies = fetch(
        (slab_far, to_d_far, to_h_far, *parts_far, from_d_far, from_h_far),
        (slab, to_d, to_h, *places, from_d, from_h),
        in_sems,
    )
    for copy in copies[:3]:
        copy.wait()
    for g in range(2):
        for p in range(8):
            for t in range(3):
                at = t * 96 + g * 48
                rows_s[p * 48:(p + 1) * 48, t * TAKE:(t + 1) * TAKE] = slab[p, at:at + 48, :]
        conv_w[g * 384:(g + 1) * 384, :] = dot(to_d[...], rows_s[...], 1, 0).astype(BF16)
    for p in range(8):
        for j in range(6):
            at = 288 + j * 16
            point_s[p * 16:(p + 1) * 16, j * TAKE:(j + 1) * TAKE] = slab[p, at:at + 16, :]
    point_w[...] = dot(to_h[...], point_s[...], 1, 0).astype(BF16)
    for copy in copies[3:8]:
        copy.wait()
    for r in range(NX):
        taps_s[r] = dot(acts[r], conv_w[...], 1, 0)
    for copy in copies[8:13]:
        copy.wait()
    for r in range(NX):
        grad_pre = dot(cts[r], point_w[...], 1, 1)
        conv_out = (
            taps_s[r, :, TAKE:2 * TAKE]
            + taps_s[(r - 1) % NX, :, :TAKE] * keep_before[r]
            + taps_s[(r + 1) % NX, :, 2 * TAKE:] * keep_after[r]
        )
        t = tanh_of(conv_out)
        cdf = 0.5 * (1.0 + t)
        inner_act[r] = (conv_out * cdf).astype(BF16)
        slope = cdf + (0.5 * conv_out) * (
            (1.0 - t * t) * (SCALE * (1.0 + 3.0 * CUBIC * (conv_out * conv_out)))
        )
        grad_s[r] = (grad_pre * slope).astype(BF16)
    for r in range(NX):
        spread_grad[r, :, :TAKE] = grad_s[(r + 1) % NX] * keep_after[r].astype(BF16)
        spread_grad[r, :, TAKE:2 * TAKE] = grad_s[r]
        spread_grad[r, :, 2 * TAKE:] = grad_s[(r - 1) % NX] * keep_before[r].astype(BF16)

    def out_part(r):
        return dot(inner_act[r], point_w[...], 1, 0).astype(BF16)

    def act_part(r):
        return dot(spread_grad[r], conv_w[...], 1, 1).astype(BF16)

    sent = []

    def send(k, value, target):
        sends[k] = value
        sent.extend(fetch((sends.at[k],), (target,), out_sems, k))

    send(0, out_part(2), out2_far)
    send(1, act_part(2), act2_far)
    send(2, out_part(3), out3_far)
    send(3, act_part(1), act1_far)
    send(4, out_part(1), out1_far)
    send(5, act_part(3), act3_far)
    send(6, out_part(0), own_far.at[0])
    send(7, act_part(0), own_far.at[1])

    for t in range(3):
        at = slice(t * TAKE, (t + 1) * TAKE)
        total = dot(spread_grad[0, :, at], acts[0], 0, 0)
        for r in range(1, NX):
            total = total + dot(spread_grad[r, :, at], acts[r], 0, 0)
        conv_g[:, at] = total.T.astype(BF16)
    copies[13].wait()
    copies[14].wait()
    for g in range(2):
        rows = dot(from_d[...], conv_g[g * 384:(g + 1) * 384, :], 1, 0).astype(BF16)
        for p in range(8):
            for t in range(3):
                grads[p, t * 96 + g * 48:t * 96 + g * 48 + 48, :] = rows[
                    p * 48:(p + 1) * 48, t * TAKE:(t + 1) * TAKE
                ]
    total = dot(inner_act[0], cts[0], 0, 0)
    for r in range(1, NX):
        total = total + dot(inner_act[r], cts[r], 0, 0)
    rows = dot(from_h[...], total.astype(BF16), 1, 0).astype(BF16)
    for p in range(8):
        for j in range(6):
            grads[p, 288 + j * 16:304 + j * 16, :] = rows[
                p * 16:(p + 1) * 16, j * TAKE:(j + 1) * TAKE
            ]
    sent.extend(fetch((grads,), (grads_far,), out_sems, 8))
    for copy in sent:
        copy.wait()


def shards(tokens, cotangent, w_conv, w_point):
    def constant(matrix):
        return jnp.asarray(matrix, BF16)

    columns, conv_rows, point_rows = column_order(), conv_rows_order(), point_rows_order()
    channels, inner = channel_order(), inner_order()

    act, ct = [None] * NX, [None] * NX
    own, act[0] = kernel_call(
        front_kernel, [shape(32, 24, TAKE), shape(ROWS, D)],
        scratch=[
            pltpu.VMEM((16, INNER), F32), pltpu.VMEM((24, TAKE), F32),
            pltpu.VMEM((3, 3, INNER), BF16), pltpu.VMEM((2, D), BF16), pltpu.VMEM((INNER, INNER), BF16),
            pltpu.VMEM((ROWS, D), BF16), pltpu.VMEM((ROWS, D), BF16), pltpu.VMEM((32, 24, TAKE), BF16),
            pltpu.SemaphoreType.DMA((4,)), pltpu.SemaphoreType.DMA((2,)),
        ],
        flops=10**7, moved=2 * 2**20, far=4, far_out=True, limit=60,
    )(w_conv, w_point, constant(columns), tokens)
    line = lax.all_to_all(own, SHEET, 0, 0)
    ct[0] = cotangent[0]
    act[3], act[1] = step_along_x(act[0], 1), step_along_x(act[0], -1)
    ct[3], ct[1] = step_along_x(ct[0], 1), step_along_x(ct[0], -1)
    def far_block(blocks):
        top, low = blocks[3][:ROWS // 2], blocks[1][ROWS // 2:]
        return step_along_x(top, 1), step_along_x(low, -1)

    line, act[1], act[3], ct[1], ct[3] = lax.optimization_barrier((line, act[1], act[3], ct[1], ct[3]))
    act[2] = far_block(act)
    ct[2] = far_block(ct)
    blocks = kernel_call(
        spread_kernel, shape(8, 384, TAKE),
        scratch=[pltpu.VMEM((384, TAKE), BF16), pltpu.VMEM((192, TAKE), F32), pltpu.VMEM((D, TAKE), F32)],
        flops=2 * 10**10, moved=2**20,
    )(line, constant(conv_rows), constant(point_rows))
    slab = lax.all_to_all(blocks, SLAB, 0, 0)
    block = shape(ROWS, D)
    grads, own, out1, act3, out2, act2, out3, act1 = kernel_call(
        middle_kernel,
        [shape(8, 384, TAKE), shape(2, ROWS, D)] + [block] * 6,
        scratch=[
            pltpu.VMEM((8, 384, TAKE), BF16), pltpu.VMEM((384, 384), BF16), pltpu.VMEM((TAKE, TAKE), BF16),
            pltpu.VMEM((NX, ROWS, D), BF16), pltpu.VMEM((NX, ROWS, D), BF16),
            pltpu.VMEM((D, 3 * TAKE), BF16), pltpu.VMEM((TAKE, D), BF16),
            pltpu.VMEM((384, 384), BF16), pltpu.VMEM((TAKE, TAKE), BF16),
            pltpu.VMEM((384, 3 * TAKE), BF16), pltpu.VMEM((TAKE, D), BF16),
            pltpu.VMEM((8, 384, TAKE), BF16),
            pltpu.VMEM((8, ROWS, D), BF16),
            pltpu.VMEM((NX, ROWS, TAKE), BF16),
            pltpu.VMEM((NX, ROWS, 3 * TAKE), BF16),
            pltpu.VMEM((NX, ROWS, 3 * TAKE), F32),
            pltpu.VMEM((NX, ROWS, TAKE), BF16),
            pltpu.VMEM((D, 3 * TAKE), BF16),
            pltpu.SemaphoreType.DMA((15,)),
            pltpu.SemaphoreType.DMA((9,)),
        ],
        flops=5 * 10**9,
        moved=12 * 2**20,
        limit=60,
        far=15,
        far_out=True,
    )(
        slab, constant(channels), constant(inner), constant(channels.T), constant(inner.T),
        act[0], act[1], act[3], *act[2], ct[0], ct[1], ct[3], *ct[2],
    )
    slab_g = lax.all_to_all(grads, SLAB, 0, 0)

    out_far, act_far = step_along_x(out2, 1), step_along_x(act2, -1)
    out_left, act_right = step_along_x(out3, -1), step_along_x(act1, 1)
    line_g = kernel_call(
        line_kernel, shape(32, 24, TAKE),
        scratch=[pltpu.VMEM((384, TAKE), BF16), pltpu.VMEM((32, 24, TAKE), F32)],
        flops=10**8, moved=2**20,
    )(slab_g, constant(conv_rows.T), constant(point_rows.T))
    out_far, act_far = lax.optimization_barrier((out_far, act_far))
    add = kernel_call(add_kernel, block, flops=3 * 10**9, moved=2**20)
    out_right = step_along_x(add(out1, out_far), 1)
    act_left = step_along_x(add(act3, act_far), -1)
    slope = kernel_call(slope_kernel, shape(ROWS, D, dtype=F32), flops=10**7, moved=2**20)(tokens[0])
    output, grad_tokens = kernel_call(
        out_kernel, [shape(ROWS, D), shape(ROWS, D)], flops=10**7, moved=4 * 2**20
    )(tokens[0], cotangent[0], slope, own, out_left, out_right, act_left, act_right)

    line_g = lax.all_to_all(line_g, SHEET, 0, 0)
    line_g, output, grad_tokens = lax.optimization_barrier((line_g, output, grad_tokens))
    conv_share, point_share = kernel_call(
        share_kernel,
        [shape(3, 3, INNER, dtype=F32), shape(2, D, dtype=F32)],
        scratch=[pltpu.VMEM((16, INNER), F32), pltpu.VMEM((24, TAKE), F32)],
        moved=2**18,
    )(line_g, constant(columns))
    return (output[None], grad_tokens[None], conv_share, point_share)


def solution(mesh):
    fine = Mesh(mesh.devices.reshape(NZ, NYH, NX, NYL, NC), AXES)
    dp, seq = ("z", "yh"), ("x", "yl", "core")
    rows = P(dp, seq, None)
    return jax.shard_map(
        shards,
        mesh=fine,
        in_specs=(rows, rows, P(None, AXES, None), P(AXES, None)),
        out_specs=(rows, rows, P(AXES, None, None), P(AXES, None)),
        check_vma=False,
    )
```

```python
import numpy as np
import jax
import jax.numpy as jnp
from jax import lax
from jax.experimental import pallas as pl
from jax.experimental.pallas import tpu as pltpu
from jax.sharding import Mesh, PartitionSpec as P

NZ, NYH, NX, NYL, NC = 8, 2, 4, 2, 2
AXES = ("z", "yh", "x", "yl", "core")
SLAB = ("yh", "yl", "core")
SHEET = ("z", "x")
ROWS, D, INNER, TAKE = 256, 768, 512, 128
BF16 = jnp.bfloat16
F32 = jnp.float32
SCALE = 0.7978845608028654
CUBIC = 0.044715


def one_hot_rows(source):
    source = np.asarray(source).reshape(-1)
    matrix = np.zeros((source.size, source.size), np.float32)
    matrix[np.arange(source.size), source] = 1.0
    return matrix


def column_order():
    return one_hot_rows([
        64 * z + 32 * yh + 8 * x + low
        for x in range(NX) for z in range(NZ) for yh in range(NYH) for low in range(8)
    ])


def conv_rows_order():
    matrix = np.zeros((144, 384), np.float32)
    for t, q, r in np.ndindex(3, 16, 3):
        matrix[t * 48 + q * 3 + r, q * 24 + t * 3 + r] = 1.0
    return matrix


def point_rows_order():
    matrix = np.zeros((96, 192), np.float32)
    for j, z, r in np.ndindex(6, NZ, 2):
        matrix[j * 16 + z * 2 + r, z * 24 + 12 + r * 6 + j] = 1.0
    return matrix


def channel_order():
    return one_hot_rows([
        ((yh * 2 + yl) * 2 + core) * 48 + z * 12 + x * 3 + r
        for z in range(4) for yh in range(NYH) for x in range(NX)
        for yl in range(NYL) for core in range(NC) for r in range(3)
    ])


def inner_order():
    return one_hot_rows([p * 16 + z * 2 + r for z in range(NZ) for p in range(8) for r in range(2)])


def step_along_x(value, step):
    return lax.ppermute(value, "x", [(i, (i + step) % NX) for i in range(NX)])


def tanh_of(values):
    return jnp.tanh(SCALE * (values + CUBIC * (values * values * values)))


def gelu_tanh(values):
    return values * (0.5 * (1.0 + tanh_of(values)))


def gelu_slope(values):
    t = tanh_of(values)
    return 0.5 * (1.0 + t) + (0.5 * values) * ((1.0 - t * t) * (SCALE * (1.0 + 3.0 * CUBIC * (values * values))))


def dot(left, right, left_dim, right_dim):
    return lax.dot_general(
        left, right, (((left_dim,), (right_dim,)), ((), ())), preferred_element_type=F32
    )


def kernel_call(body, out_shapes, scratch=(), flops=0, moved=0, limit=8, far=0, far_out=False):
    many = isinstance(out_shapes, (list, tuple))
    vmem, hbm = pl.BlockSpec(memory_space=pltpu.VMEM), pl.BlockSpec(memory_space=pltpu.HBM)
    out_spec = hbm if far_out else vmem

    def call(*operands):
        return pl.pallas_call(
            body,
            out_shape=out_shapes,
            in_specs=[vmem] * (len(operands) - far) + [hbm] * far,
            out_specs=[out_spec] * len(out_shapes) if many else out_spec,
            scratch_shapes=list(scratch),
            compiler_params=pltpu.CompilerParams(vmem_limit_bytes=limit * 2**20),
            cost_estimate=pl.CostEstimate(flops=flops, bytes_accessed=moved, transcendentals=0),
        )(*operands)

    return call


def shape(*dims, dtype=BF16):
    return jax.ShapeDtypeStruct(dims, dtype)


def fetch(sources, targets, sems, first=0):
    copies = [
        pltpu.make_async_copy(source, target, sems.at[first + k])
        for k, (source, target) in enumerate(zip(sources, targets))
    ]
    for copy in copies:
        copy.start()
    return copies


def front_kernel(
    w_conv_far, w_point_far, order_far, tokens_far,
    out_far, act_far,
    rows_s, block_s, w_conv, w_point, order, tokens, act, own_s, in_sems, out_sems,
):
    copies = fetch(
        (tokens_far.at[0], w_conv_far, w_point_far, order_far),
        (tokens, w_conv, w_point, order),
        in_sems,
    )
    for copy in copies[1:]:
        copy.wait()
    rows_s[...] = jnp.zeros_like(rows_s)
    for t in range(3):
        rows_s[t * 3:(t + 1) * 3, :] = w_conv[t].astype(F32)
    parted = dot(rows_s[...].astype(BF16), order[...], 1, 1)
    block_s[...] = jnp.zeros_like(block_s)
    point = w_point[...].astype(F32)
    for r in range(2):
        for j in range(6):
            block_s[pl.ds(12 + r * 6 + j, 1), :] = point[r:r + 1, j * TAKE:(j + 1) * TAKE]
    for x in range(NX):
        block_s[:9, :] = parted[:9, x * TAKE:(x + 1) * TAKE]
        block = block_s[...].astype(BF16)
        for z in range(NZ):
            own_s[z * NX + x] = block
    sent = fetch((own_s,), (out_far,), out_sems)
    copies[0].wait()
    for k in range(4):
        at = slice(k * 64, (k + 1) * 64)
        act[at, :] = gelu_tanh(tokens[at, :].astype(F32)).astype(BF16)
    sent += fetch((act,), (act_far,), out_sems, 1)
    for copy in sent:
        copy.wait()


def share_kernel(line, order, conv_share, point_share, rows_s, sum_s):
    me = lax.axis_index("x")
    rows_s[...] = jnp.zeros_like(rows_s)
    for x in range(NX):
        total = line[x].astype(F32)
        for z in range(1, NZ):
            total = total + line[z * NX + x].astype(F32)
        sum_s[...] = total
        rows_s[:9, x * TAKE:(x + 1) * TAKE] = sum_s[:9, :]
    total = line[me].astype(F32)
    for z in range(1, NZ):
        total = total + line[z * NX + me].astype(F32)
    sum_s[...] = total
    for r in range(2):
        for j in range(6):
            point_share[pl.ds(r, 1), j * TAKE:(j + 1) * TAKE] = sum_s[pl.ds(12 + r * 6 + j, 1), :]
    rows = rows_s[...]
    high = rows.astype(BF16)
    low = (rows - high.astype(F32)).astype(BF16)
    joined = dot(high, order[...], 1, 0) + dot(low, order[...], 1, 0)
    for t in range(3):
        for r in range(3):
            conv_share[r, pl.ds(t, 1), :] = joined[t * 3 + r:t * 3 + r + 1, :]


def slope_kernel(tokens, slope):
    for k in range(4):
        at = slice(k * 64, (k + 1) * 64)
        slope[at, :] = gelu_slope(tokens[at, :].astype(F32))


def add_kernel(mine, other, out):
    out[...] = (mine[...].astype(F32) + other[...].astype(F32)).astype(BF16)


def out_kernel(
    tokens, cotangent, slope, own, out_left, out_right, act_left, act_right, output, grad_tokens
):
    for k in range(4):
        at = slice(k * 64, (k + 1) * 64)
        output[at, :] = (
            tokens[at, :].astype(F32) + own[0, at, :].astype(F32)
            + out_left[at, :].astype(F32) + out_right[at, :].astype(F32)
        ).astype(BF16)
        grad_act = own[1, at, :].astype(F32) + act_right[at, :].astype(F32) + act_left[at, :].astype(F32)
        grad_tokens[at, :] = (cotangent[at, :].astype(F32) + grad_act * slope[at, :]).astype(BF16)


def spread_kernel(line, conv_order, point_order, out, block_s, mine_s, all_s):
    me = lax.axis_index("x")
    for q in range(32):
        all_s[q * 24:(q + 1) * 24, :] = line[q].astype(F32)
    for z in range(NZ):
        mine_s[z * 24:(z + 1) * 24, :] = line[z * NX + me].astype(F32)
    for g in range(2):
        rows = dot(conv_order[...], all_s[g * 384:(g + 1) * 384, :].astype(BF16), 1, 0).astype(BF16)
        for t in range(3):
            block_s[t * 96 + g * 48:t * 96 + g * 48 + 48, :] = rows[t * 48:(t + 1) * 48]
    block_s[288:, :] = dot(point_order[...], mine_s[...].astype(BF16), 1, 0).astype(BF16)
    for p in range(8):
        out[p] = block_s[...]


def line_kernel(slab, conv_order, point_order, out, block_s, all_s):
    me = lax.axis_index("x")
    total = slab[0].astype(F32)
    for p in range(1, 8):
        total = total + slab[p].astype(F32)
    block_s[...] = total.astype(BF16)
    for g in range(2):
        rows = dot(conv_order[:, :48], block_s[g * 48:g * 48 + 48, :], 1, 0)
        for t in (1, 2):
            rows = rows + dot(
                conv_order[:, t * 48:(t + 1) * 48], block_s[t * 96 + g * 48:t * 96 + g * 48 + 48, :], 1, 0
            )
        for q in range(16):
            all_s[g * 16 + q] = rows[q * 24:(q + 1) * 24]
    rows = dot(point_order[...], block_s[288:, :], 1, 0)
    for z in range(NZ):
        all_s[z * NX + me] += rows[z * 24:(z + 1) * 24]
    for q in range(32):
        out[q] = all_s[q].astype(BF16)


def middle_kernel(
    slab_far, to_d_far, to_h_far, from_d_far, from_h_far, *refs,
):
    parts_far, refs = refs[:10], refs[10:]
    grads_far, own_far, out1_far, act3_far, out2_far, act2_far, out3_far, act1_far = refs[:8]
    (
        slab, to_d, to_h, acts, cts, conv_w, point_w, from_d, from_h, rows_s, point_s, grads, sends,
        inner_act, spread_grad, taps_s, grad_s, conv_g, in_sems, out_sems,
    ) = refs[8:]
    me = lax.axis_index("x")
    place = [lax.rem(me + r, NX) for r in range(NX)]
    keep_before = [(p != 0).astype(F32) for p in place]
    keep_after = [(p != NX - 1).astype(F32) for p in place]
    top, low = slice(0, ROWS // 2), slice(ROWS // 2, ROWS)
    places = [
        full.at[r, at] for full in (acts, cts)
        for r, at in ((0, slice(None)), (1, slice(None)), (3, slice(None)), (2, top), (2, low))
    ]
    copies = fetch(
        (slab_far, to_d_far, to_h_far, *parts_far, from_d_far, from_h_far),
        (slab, to_d, to_h, *places, from_d, from_h),
        in_sems,
    )
    for copy in copies[:3]:
        copy.wait()
    for g in range(2):
        for p in range(8):
            for t in range(3):
                at = t * 96 + g * 48
                rows_s[p * 48:(p + 1) * 48, t * TAKE:(t + 1) * TAKE] = slab[p, at:at + 48, :]
        conv_w[g * 384:(g + 1) * 384, :] = dot(to_d[...], rows_s[...], 1, 0).astype(BF16)
    for p in range(8):
        for j in range(6):
            at = 288 + j * 16
            point_s[p * 16:(p + 1) * 16, j * TAKE:(j + 1) * TAKE] = slab[p, at:at + 16, :]
    point_w[...] = dot(to_h[...], point_s[...], 1, 0).astype(BF16)
    for r, arrived in ((0, copies[3:4]), (1, copies[4:5]), (3, copies[5:6]), (2, copies[6:8])):
        for copy in arrived:
            copy.wait()
        taps_s[r] = dot(acts[r], conv_w[...], 1, 0)
    for copy in copies[8:13]:
        copy.wait()
    for r in range(NX):
        grad_pre = dot(cts[r], point_w[...], 1, 1)
        conv_out = (
            taps_s[r, :, TAKE:2 * TAKE]
            + taps_s[(r - 1) % NX, :, :TAKE] * keep_before[r]
            + taps_s[(r + 1) % NX, :, 2 * TAKE:] * keep_after[r]
        )
        t = tanh_of(conv_out)
        cdf = 0.5 * (1.0 + t)
        inner_act[r] = (conv_out * cdf).astype(BF16)
        slope = cdf + (0.5 * conv_out) * (
            (1.0 - t * t) * (SCALE * (1.0 + 3.0 * CUBIC * (conv_out * conv_out)))
        )
        grad_s[r] = (grad_pre * slope).astype(BF16)
    for r in range(NX):
        spread_grad[r, :, :TAKE] = grad_s[(r + 1) % NX] * keep_after[r].astype(BF16)
        spread_grad[r, :, TAKE:2 * TAKE] = grad_s[r]
        spread_grad[r, :, 2 * TAKE:] = grad_s[(r - 1) % NX] * keep_before[r].astype(BF16)

    def out_part(r):
        return dot(inner_act[r], point_w[...], 1, 0).astype(BF16)

    def act_part(r):
        return dot(spread_grad[r], conv_w[...], 1, 1).astype(BF16)

    sent = []

    def send(k, value, target):
        sends[k] = value
        sent.extend(fetch((sends.at[k],), (target,), out_sems, k))

    send(0, out_part(2), out2_far)
    send(1, act_part(2), act2_far)
    send(2, out_part(3), out3_far)
    send(3, act_part(1), act1_far)
    send(4, out_part(1), out1_far)
    send(5, act_part(3), act3_far)
    send(6, out_part(0), own_far.at[0])
    send(7, act_part(0), own_far.at[1])

    for t in range(3):
        at = slice(t * TAKE, (t + 1) * TAKE)
        total = dot(spread_grad[0, :, at], acts[0], 0, 0)
        for r in range(1, NX):
            total = total + dot(spread_grad[r, :, at], acts[r], 0, 0)
        conv_g[:, at] = total.T.astype(BF16)
    copies[13].wait()
    copies[14].wait()
    for g in range(2):
        rows = dot(from_d[...], conv_g[g * 384:(g + 1) * 384, :], 1, 0).astype(BF16)
        for p in range(8):
            for t in range(3):
                grads[p, t * 96 + g * 48:t * 96 + g * 48 + 48, :] = rows[
                    p * 48:(p + 1) * 48, t * TAKE:(t + 1) * TAKE
                ]
    sent.extend(fetch((grads.at[:, :288],), (grads_far.at[:, :288],), out_sems, 8))
    total = dot(inner_act[0], cts[0], 0, 0)
    for r in range(1, NX):
        total = total + dot(inner_act[r], cts[r], 0, 0)
    rows = dot(from_h[...], total.astype(BF16), 1, 0).astype(BF16)
    for p in range(8):
        for j in range(6):
            grads[p, 288 + j * 16:304 + j * 16, :] = rows[
                p * 16:(p + 1) * 16, j * TAKE:(j + 1) * TAKE
            ]
    sent.extend(fetch((grads.at[:, 288:],), (grads_far.at[:, 288:],), out_sems, 9))
    for copy in sent:
        copy.wait()


def shards(tokens, cotangent, w_conv, w_point):
    def constant(matrix):
        return jnp.asarray(matrix, BF16)

    columns, conv_rows, point_rows = column_order(), conv_rows_order(), point_rows_order()
    channels, inner = channel_order(), inner_order()

    act, ct = [None] * NX, [None] * NX
    own, act[0] = kernel_call(
        front_kernel, [shape(32, 24, TAKE), shape(ROWS, D)],
        scratch=[
            pltpu.VMEM((16, INNER), F32), pltpu.VMEM((24, TAKE), F32),
            pltpu.VMEM((3, 3, INNER), BF16), pltpu.VMEM((2, D), BF16), pltpu.VMEM((INNER, INNER), BF16),
            pltpu.VMEM((ROWS, D), BF16), pltpu.VMEM((ROWS, D), BF16), pltpu.VMEM((32, 24, TAKE), BF16),
            pltpu.SemaphoreType.DMA((4,)), pltpu.SemaphoreType.DMA((2,)),
        ],
        flops=10**7, moved=2 * 2**20, far=4, far_out=True, limit=60,
    )(w_conv, w_point, constant(columns), tokens)
    line = lax.all_to_all(own, SHEET, 0, 0)
    ct[0] = cotangent[0]
    act[3], act[1] = step_along_x(act[0], 1), step_along_x(act[0], -1)
    ct[3], ct[1] = step_along_x(ct[0], 1), step_along_x(ct[0], -1)
    def far_block(blocks):
        top, low = blocks[3][:ROWS // 2], blocks[1][ROWS // 2:]
        return step_along_x(top, 1), step_along_x(low, -1)

    line, act[1], act[3], ct[1], ct[3] = lax.optimization_barrier((line, act[1], act[3], ct[1], ct[3]))
    act[2] = far_block(act)
    ct[2] = far_block(ct)
    blocks = kernel_call(
        spread_kernel, shape(8, 384, TAKE),
        scratch=[pltpu.VMEM((384, TAKE), BF16), pltpu.VMEM((192, TAKE), F32), pltpu.VMEM((D, TAKE), F32)],
        flops=2 * 10**10, moved=2**20,
    )(line, constant(conv_rows), constant(point_rows))
    slab = lax.all_to_all(blocks, SLAB, 0, 0)
    block = shape(ROWS, D)
    grads, own, out1, act3, out2, act2, out3, act1 = kernel_call(
        middle_kernel,
        [shape(8, 384, TAKE), shape(2, ROWS, D)] + [block] * 6,
        scratch=[
            pltpu.VMEM((8, 384, TAKE), BF16), pltpu.VMEM((384, 384), BF16), pltpu.VMEM((TAKE, TAKE), BF16),
            pltpu.VMEM((NX, ROWS, D), BF16), pltpu.VMEM((NX, ROWS, D), BF16),
            pltpu.VMEM((D, 3 * TAKE), BF16), pltpu.VMEM((TAKE, D), BF16),
            pltpu.VMEM((384, 384), BF16), pltpu.VMEM((TAKE, TAKE), BF16),
            pltpu.VMEM((384, 3 * TAKE), BF16), pltpu.VMEM((TAKE, D), BF16),
            pltpu.VMEM((8, 384, TAKE), BF16),
            pltpu.VMEM((8, ROWS, D), BF16),
            pltpu.VMEM((NX, ROWS, TAKE), BF16),
            pltpu.VMEM((NX, ROWS, 3 * TAKE), BF16),
            pltpu.VMEM((NX, ROWS, 3 * TAKE), F32),
            pltpu.VMEM((NX, ROWS, TAKE), BF16),
            pltpu.VMEM((D, 3 * TAKE), BF16),
            pltpu.SemaphoreType.DMA((15,)),
            pltpu.SemaphoreType.DMA((10,)),
        ],
        flops=5 * 10**9,
        moved=12 * 2**20,
        limit=60,
        far=15,
        far_out=True,
    )(
        slab, constant(channels), constant(inner), constant(channels.T), constant(inner.T),
        act[0], act[1], act[3], *act[2], ct[0], ct[1], ct[3], *ct[2],
    )
    slab_g = lax.all_to_all(grads, SLAB, 0, 0)

    out_far, act_far = step_along_x(out2, 1), step_along_x(act2, -1)
    out_left, act_right = step_along_x(out3, -1), step_along_x(act1, 1)
    line_g = kernel_call(
        line_kernel, shape(32, 24, TAKE),
        scratch=[pltpu.VMEM((384, TAKE), BF16), pltpu.VMEM((32, 24, TAKE), F32)],
        flops=10**8, moved=2**20,
    )(slab_g, constant(conv_rows.T), constant(point_rows.T))
    out_far, act_far = lax.optimization_barrier((out_far, act_far))
    add = kernel_call(add_kernel, block, flops=3 * 10**9, moved=2**20)
    out_right = step_along_x(add(out1, out_far), 1)
    act_left = step_along_x(add(act3, act_far), -1)
    slope = kernel_call(slope_kernel, shape(ROWS, D, dtype=F32), flops=10**7, moved=2**20)(tokens[0])
    output, grad_tokens = kernel_call(
        out_kernel, [shape(ROWS, D), shape(ROWS, D)], flops=10**7, moved=4 * 2**20
    )(tokens[0], cotangent[0], slope, own, out_left, out_right, act_left, act_right)

    line_g = lax.all_to_all(line_g, SHEET, 0, 0)
    line_g, output, grad_tokens = lax.optimization_barrier((line_g, output, grad_tokens))
    conv_share, point_share = kernel_call(
        share_kernel,
        [shape(3, 3, INNER, dtype=F32), shape(2, D, dtype=F32)],
        scratch=[pltpu.VMEM((16, INNER), F32), pltpu.VMEM((24, TAKE), F32)],
        moved=2**18,
    )(line_g, constant(columns))
    return (output[None], grad_tokens[None], conv_share, point_share)


def solution(mesh):
    fine = Mesh(mesh.devices.reshape(NZ, NYH, NX, NYL, NC), AXES)
    dp, seq = ("z", "yh"), ("x", "yl", "core")
    rows = P(dp, seq, None)
    return jax.shard_map(
        shards,
        mesh=fine,
        in_specs=(rows, rows, P(None, AXES, None), P(AXES, None)),
        out_specs=(rows, rows, P(AXES, None, None), P(AXES, None)),
        check_vma=False,
    )
```
